512 devices in a mesh: cand: 16 (over z, core), fsdp: 16 (over x_hi, y), prompt: 2 (over x_lo).
Axes of the slice: x: 4 (x_hi: 2, x_lo: 2; x = x_hi * 2 + x_lo), y: 8, z: 8, core: 2. Of those that a mesh axis runs over, the one named last changes fastest.
Arguments:
- hidden: bfloat16 [2, 16, 8192, 4608], P('prompt', 'cand', 'fsdp'), may hold values from -12 to 12
- lengths: int32 [2, 16], P('prompt', 'cand'), may hold values from 2048 to 8192, as said below
- starts: int32 [2, 16], P('prompt', 'cand'), may hold values from 0 to 1023
- ranking: int32 [2, 16], P('prompt'), may hold values from 0 to 15, each once within a row
- down_w: bfloat16 [96, 4608], P(None, 'fsdp'), may hold values from -0.09375 to 0.09375
- up_w: bfloat16 [96, 4608], P(None, 'fsdp'), may hold values from -0.625 to 0.625
- gain: bfloat16 [4608], P('fsdp'), may hold values from 0.5 to 1.5
- head: bfloat16 [4608], P('fsdp'), may hold values from -1 to 1
Outputs:
- list_loss: float32 [2], P('prompt')
- down_grad: float32 [96, 4608], P(None, 'fsdp')
- up_grad: float32 [96, 4608], P(None, 'fsdp')
- gain_grad: float32 [4608], P('fsdp')
- head_grad: float32 [4608], P('fsdp')
The draws below stay inside these ranges and needn't reach their ends.
Inputs may be any that keep to these rules, and one draw needn't show every extreme that they name: `lengths`: every prompt has a candidate of length 8192.
All inputs are finite; a program needn't handle non-finite values.
Results may differ from the reference program's by a relative error of at most 0.0003.
Values may be sent and summed in bfloat16 or wider, within the bound.
No kernel may reach another device: no remote copies, remote signals or barrier semaphores. Data moves between devices by JAX's collectives and lax.ppermute only.
A program may use at most 64 MiB of HBM per device.

```python
import math
import jax
import jax.numpy as jnp
from jax import lax

D = 4608
R = 96
LEN = 8192
CANDS = 16
PROMPTS = 2


def draw_hidden(key, part):
    key = jax.random.fold_in(key, 11)
    key_offset, key_noise, key_scale = jax.random.split(key, 3)
    offset = jax.random.normal(key_offset, (PROMPTS, CANDS, 1, D), jnp.float32)
    spread = jnp.exp(jax.random.uniform(key_scale, (PROMPTS, CANDS, LEN, 1), jnp.float32, 0.0, math.log(10.0)))
    noise = jax.random.normal(key_noise, (PROMPTS, CANDS, LEN, D), jnp.float32)
    values = offset + 0.5 * noise * spread
    return jnp.clip(values, -12.0, 12.0).astype(jnp.bfloat16)


def draw_head(key, part):
    key = jax.random.fold_in(key, 12)
    values = jax.random.normal(key, (D,), jnp.float32) * math.sqrt(8.0 / D)
    return jnp.clip(values, -1.0, 1.0).astype(jnp.bfloat16)


def draw_lengths(key, part):
    key = jax.random.fold_in(key, 13)
    key_base, key_which = jax.random.split(key)
    base = jax.random.randint(key_base, (PROMPTS, CANDS), LEN // 4, LEN + 1, jnp.int32)
    which = jax.random.randint(key_which, (PROMPTS, 1), 0, CANDS, jnp.int32)
    column = jnp.arange(CANDS, dtype=jnp.int32)[None, :]
    return jnp.where(column == which, LEN, base).astype(jnp.int32)


def place_ends(result, own_key, low, largest):
    longest = result.shape.index(max(result.shape))
    spots = []
    for shift in (0, 1):
        where = [jax.random.randint(jax.random.fold_in(own_key, axis), (), 0, length) for axis, length in enumerate(result.shape)]
        where[longest] = (where[longest] + shift) % result.shape[longest]
        spots.append(tuple(where))
    return result.at[spots[0]].set(low).at[spots[1]].set(largest)


def steps_of(stream_key, dims, cuts, least, high):
    def one(axis_at, blocks):
        draws = jax.random.uniform(jax.random.fold_in(jax.random.fold_in(stream_key, 6), axis_at), (blocks,), jnp.float32, least / len(cuts), high / len(cuts))
        return jnp.repeat(jnp.exp(draws), dims[axis_at] // blocks).reshape((-1,) + (1,) * (len(dims) - axis_at - 1))

    level = one(*cuts[0])
    for cut in cuts[1:]:
        level = level * one(*cut)
    return level


def bell_draw(stream_key, extent, scale, most, cuts=(), held_as=jnp.bfloat16):
    entries = jax.random.normal(stream_key, extent, jnp.float32) * scale
    if len(cuts) > 0:
        entries = steps_of(stream_key, extent, cuts, -0.22, 0.18) * entries
    return jnp.clip(entries, min=-most, max=most).astype(held_as)


def setup_inputs(seed: int = 0) -> dict:
    splits = jax.random.split(jax.random.key(seed), 9)
    return {
        "hidden": draw_hidden(jax.random.fold_in(splits[8], 71), 0),
        "lengths": draw_lengths(jax.random.fold_in(splits[8], 71), 0),
        "starts": place_ends(jax.random.randint(splits[2], (PROMPTS, CANDS), 0, LEN // 8), jax.random.fold_in(splits[2], 1), 0, (LEN // 8) - 1).astype(jnp.int32),
        "ranking": jax.vmap(lambda own: jax.random.permutation(own, CANDS))(jax.random.split(splits[3], PROMPTS)).reshape((PROMPTS, CANDS)).astype(jnp.int32),
        "down_w": bell_draw(splits[4], (R, D), D ** -0.5, 0.09375, ((1, 16),)),
        "up_w": bell_draw(splits[5], (R, D), R ** -0.5, 0.625, ((1, 16),)),
        "gain": jnp.clip(1.0 + 0.1 * jax.random.normal(splits[6], (D,), jnp.float32), 0.5, 1.5).astype(jnp.bfloat16),
        "head": draw_head(jax.random.fold_in(splits[8], 71), 0),
    }


loss_scale = 256.0

def token_forward(rows, down_full, up_full, gain_f, head_f):
    pre = lax.dot_general(rows, down_full, (((1,), (1,)), ((), ())), preferred_element_type=jnp.float32)
    act = jax.nn.silu(pre).astype(jnp.bfloat16)
    mixed = rows.astype(jnp.float32) + jnp.dot(act, up_full, preferred_element_type=jnp.float32)
    inv = lax.rsqrt(lax.optimization_barrier(jnp.mean(mixed * mixed, axis=-1, keepdims=True)) + 1e-06)
    scaled = mixed * inv
    score = lax.optimization_barrier(jnp.sum(scaled * (gain_f * head_f)[None, :], axis=-1))
    return (pre, act, scaled, inv, score)

def token_backward(rows, up_full, gain_f, head_f, pre, act, scaled, inv, weight):
    pooled = jnp.dot(weight, scaled, precision=lax.Precision.HIGHEST)
    head_grad = gain_f * pooled
    gain_grad = head_f * pooled
    upper = weight[:, None] * (head_f * gain_f)[None, :]
    mixed_grad = (inv * (upper - scaled * lax.optimization_barrier(jnp.mean(upper * scaled, axis=-1, keepdims=True)))).astype(jnp.bfloat16)
    up_grad = lax.dot_general(act, mixed_grad, (((0,), (0,)), ((), ())), preferred_element_type=jnp.float32)
    back = lax.dot_general(mixed_grad, up_full, (((1,), (1,)), ((), ())), preferred_element_type=jnp.float32)
    sigma = jax.nn.sigmoid(pre)
    pre_grad = (back * sigma * (1.0 + pre * (1.0 - sigma))).astype(jnp.bfloat16)
    down_grad = lax.dot_general(pre_grad, rows, (((0,), (0,)), ((), ())), preferred_element_type=jnp.float32)
    return (down_grad, up_grad, gain_grad, head_grad)

def ranked_loss(rewards, order):
    ranked = jnp.take(rewards, order)
    width = ranked.shape[0]
    index = lax.iota(jnp.int32, width)
    later = index[None, :] >= index[:, None]
    top = lax.stop_gradient(lax.optimization_barrier(jnp.max(jnp.where(later, ranked[None, :], -1e+30), axis=1)))
    diff = jnp.where(later, ranked[None, :] - top[:, None], -10000.0)
    return jnp.sum(top + jnp.log(lax.optimization_barrier(jnp.sum(jnp.exp(diff), axis=1))) - ranked)

def prompt_slope(rewards, order):
    loss, pull = jax.vjp(lambda v: ranked_loss(v, order), rewards)
    return (loss, pull(jnp.ones_like(loss))[0])

def reference(hidden, lengths, starts, ranking, down_w, up_w, gain, head):
    gain_f = gain.astype(jnp.float32)
    head_f = head.astype(jnp.float32)
    flat_hidden = hidden.reshape(PROMPTS * CANDS, LEN, D)
    flat_len = lengths.reshape(PROMPTS * CANDS)
    flat_start = starts.reshape(PROMPTS * CANDS)
    positions = lax.iota(jnp.int32, LEN)

    def score_one(item):
        rows, length, start = item
        score = token_forward(rows, down_w, up_w, gain_f, head_f)[4]
        valid = (positions >= start) & (positions < length)
        count = (length - start).astype(jnp.float32)
        return jnp.sum(jnp.where(valid, score, 0.0)) / count
    rewards = lax.map(score_one, (flat_hidden, flat_len, flat_start)).reshape(PROMPTS, CANDS)
    losses, slopes = jax.vmap(prompt_slope)(rewards, ranking)
    flat_slope = slopes.reshape(PROMPTS * CANDS)

    def accumulate(carry, item):
        rows, length, start, slope = item
        pre, act, scaled, inv, score = token_forward(rows, down_w, up_w, gain_f, head_f)
        valid = (positions >= start) & (positions < length)
        count = (length - start).astype(jnp.float32)
        weight = jnp.where(valid, loss_scale * slope / count, 0.0)
        terms = token_backward(rows, up_w, gain_f, head_f, pre, act, scaled, inv, weight)
        return (tuple((a + b for a, b in zip(carry, terms))), None)
    init = (jnp.zeros((R, D), jnp.float32), jnp.zeros((R, D), jnp.float32), jnp.zeros((D,), jnp.float32), jnp.zeros((D,), jnp.float32))
    grads, unused = lax.scan(accumulate, init, (flat_hidden, flat_len, flat_start, flat_slope))
    return (losses, grads[0], grads[1], grads[2], grads[3])
```

```python
import functools

import jax
import jax.numpy as jnp
from jax import lax
from jax.experimental import pallas as pl
from jax.experimental.pallas import tpu as pltpu
from jax.sharding import PartitionSpec as P

loss_scale = 256.0
D = 4608
R = 96
TOK = 512
NB = 16
BW = 288
CH = 512
STEPS = 32760.0
FINE = 60000.0
TINY = 1e-36
f32 = jnp.float32
bf16 = jnp.bfloat16
VMEM = pl.BlockSpec(memory_space=pltpu.VMEM)
SMEM = pl.BlockSpec(memory_space=pltpu.SMEM)


def mm(a, b, ca, cb):
    return lax.dot_general(a, b, (((ca,), (cb,)), ((), ())), preferred_element_type=f32)


def halves(v):
    hi = v.astype(bf16)
    return hi, (v - hi.astype(f32)).astype(bf16)


def lanes(shape):
    return lax.broadcasted_iota(jnp.int32, shape, len(shape) - 1)


def level(most):
    return jnp.ceil(jnp.log2(jnp.maximum(most, TINY)) * 8.0)


def coded(v, e):
    return jnp.round(v * jnp.exp2(e * -0.125) * STEPS).astype(jnp.int32)


def local_kernel(info, x_ref, mine_ref, other_ref, out_ref, w_ref, ss_ref, g_ref, p_ref):
    start, length, first, core = info[0], info[1], info[2], info[3]

    @pl.when(core == 0)
    def _():
        w_ref[:, :128] = mine_ref[...]
        w_ref[:, 128:] = other_ref[...]

    @pl.when(core != 0)
    def _():
        w_ref[:, :128] = other_ref[...]
        w_ref[:, 128:] = mine_ref[...]

    def square(i, carry):
        rows = x_ref[pl.ds(pl.multiple_of(i * 16, 16), 16), :].astype(f32)
        ss_ref[pl.ds(pl.multiple_of(i * 16, 16), 16), :] = jnp.sum(rows * rows, axis=1, keepdims=True)
        return carry

    lax.fori_loop(0, TOK // 16, square, 0)

    prod = mm(x_ref[...], w_ref[...], 1, 0)
    gram = mm(w_ref[...], w_ref[...], 0, 0)
    pre = prod[:, :128]
    x_up = prod[:, 128:]
    lane = lanes((TOK, 128))
    unit = lane < R
    sig = 1.0 / (1.0 + jnp.exp(-pre))
    act_b = jnp.where(unit, pre * sig, 0.0).astype(bf16)
    act = act_b.astype(f32)
    g_hi, g_lo = halves(gram[128:, :])
    through = mm(act_b, g_hi, 1, 0) + mm(act_b, g_lo, 1, 0)
    m_left = pre + through[:, :128]
    m_up = x_up + through[:, 128:]
    m_head = jnp.sum(jnp.where((lane == R) | (lane == R + 1), m_left, 0.0), axis=1, keepdims=True)
    m_sq = ss_ref[...] + jnp.sum(act * (x_up + m_up), axis=1, keepdims=True)
    inv = lax.rsqrt(jnp.maximum(m_sq, 0.0) * (1.0 / D) + 1e-06)
    score = inv * m_head
    count = (length - start).astype(f32)
    pos = first + lax.broadcasted_iota(jnp.int32, (TOK, 1), 0)
    valid = (pos >= start) & (pos < length)
    part = jnp.sum(jnp.where(valid, score, 0.0), axis=0, keepdims=True) / count
    weight = jnp.where(valid, loss_scale / count, 0.0)
    alpha = inv * weight
    beta = inv * inv * weight * score * (1.0 / D)
    up_head = gram[R : R + 1, 128:] + gram[R + 1 : R + 2, 128:]
    back = alpha * up_head - beta * m_up
    pre_grad = back * sig * (1.0 + pre * (1.0 - sig))
    nab = -(act * beta)
    left = jnp.where(unit, pre_grad, pltpu.roll(nab, 32, 1))
    right = jnp.where(lane < 64, nab, pltpu.roll(nab, 64, 1))
    lhs = jnp.concatenate([left, right], axis=1).astype(bf16)
    a_left = jnp.where(unit, 0.0, pltpu.roll(act, 32, 1))
    a_right = jnp.where(lane < 64, act, pltpu.roll(act, 64, 1))
    u_row = jnp.sum(alpha * jnp.concatenate([a_left, a_right], axis=1), axis=0, keepdims=True)
    v_row = jnp.sum(alpha * act, axis=0, keepdims=True)
    low = mm(act_b, lhs, 0, 0)
    low = jnp.where(lanes((128, 256)) < R, 0.0, low)
    row = lax.broadcasted_iota(jnp.int32, (128, 256), 0)
    top = jnp.where((row == R) | (row == R + 1), u_row, 0.0)
    c_hi, c_lo = halves(jnp.concatenate([top, low], axis=0))
    for i in range(D // CH):
        cut = slice(i * CH, (i + 1) * CH)
        w = w_ref[cut, :]
        g_ref[cut, :] = mm(x_ref[:, cut], lhs, 0, 0) + (mm(w, c_hi, 1, 0) + mm(w, c_lo, 1, 0))

    al_hi = alpha.astype(bf16).astype(f32)
    al_lo = alpha - al_hi
    al = jnp.where(lane == 0, al_hi, jnp.where(lane == 1, al_lo, 0.0))
    al = jnp.transpose(al)[:16].astype(bf16)
    v_hi = v_row.astype(bf16).astype(f32)
    row = lax.broadcasted_iota(jnp.int32, (16, 128), 0)
    vv = jnp.where(row == 0, v_hi, jnp.where(row == 1, v_row - v_hi, 0.0)).astype(bf16)
    pooled = mm(al, x_ref[...], 1, 0) + mm(vv, w_ref[:, 128:], 1, 1)
    p_ref[:, D:] = jnp.zeros((8, 256), f32)
    p_ref[:, :D] = jnp.broadcast_to(pooled[0:1] + pooled[1:2], (8, D))

    s_e = level(jnp.abs(part))
    s_v = part * jnp.exp2(s_e * -0.125) * STEPS
    s_hi = jnp.round(s_v)
    s_lo = jnp.round((s_v - s_hi) * FINE)
    one = lanes((1, 128))
    s_row = jnp.where(one == 0, s_e, jnp.where(one == 1, s_hi, jnp.where(one == 2, s_lo, 0.0))).astype(jnp.int32)
    for j in range(NB):
        a = g_ref[j * BW : (j + 1) * BW, :128]
        b0 = g_ref[j * BW : j * BW + BW // 2, 128:]
        b1 = g_ref[j * BW + BW // 2 : (j + 1) * BW, 128:]
        b = jnp.where(lanes((BW // 2, 128)) < 64, b0, b1)
        a_e = level(jnp.max(jnp.abs(a), axis=0, keepdims=True))
        b_e = level(jnp.max(jnp.abs(b), axis=0, keepdims=True))
        out_ref[j, :BW, :] = coded(a, a_e).astype(jnp.int16)
        out_ref[j, BW : BW + BW // 2, :] = coded(b, b_e).astype(jnp.int16)
        base = j * BW // 128 * 128
        window = p_ref[:, base : base + 512]
        off = j * BW - base
        if off:
            window = pltpu.roll(window, 512 - off, 1)
        window = jnp.where(lanes((8, 512)) < BW, window, 0.0)
        p_e = level(jnp.max(jnp.abs(window), axis=1, keepdims=True))
        p_q = coded(window, p_e)
        at = lax.broadcasted_iota(jnp.int32, (16, 128), 0)
        rows = (
            a_e.astype(jnp.int32),
            b_e.astype(jnp.int32),
            p_q[0:1, :128],
            p_q[0:1, 128:256],
            p_q[0:1, 256:384],
            jnp.broadcast_to(p_e[0:1].astype(jnp.int32), (1, 128)),
            s_row,
        )
        meta = jnp.zeros((16, 128), jnp.int32)
        for k, r in enumerate(rows):
            meta = jnp.where(at == k, r, meta)
        out_ref[j, BW + BW // 2 :, :] = meta.astype(jnp.int16)


def block_kernel(info, ranking, q_ref, out_ref):
    mine = info[4]
    place = jnp.int32(0)
    for k in range(16):
        place = jnp.where(ranking[0, k] == mine, jnp.int32(k), place)
    half = BW + BW // 2
    parts = [q_ref[s, half:, :].astype(jnp.int32).astype(f32) for s in range(NB)]
    scale = [jnp.exp2(m * 0.125) for m in parts]
    pooled = [jnp.zeros((1, 128), f32) for _ in range(3)]
    reward = jnp.zeros((1, 128), f32)
    one = lanes((1, 128))
    for s in range(NB):
        m, e = parts[s], scale[s] * (1.0 / STEPS)
        for k in range(3):
            pooled[k] = pooled[k] + m[2 + k : 3 + k] * e[5:6]
        told = jnp.where(one == 1, m[6:7], jnp.where(one == 2, m[6:7] * (1.0 / FINE), 0.0))
        told = jnp.sum(told, axis=1, keepdims=True)
        by = jnp.sum(jnp.where(one == 0, e[6:7], 0.0), axis=1, keepdims=True)
        reward = reward + told * by
    at = lax.broadcasted_iota(jnp.int32, (16, 128), 0)
    tail = jnp.zeros((16, 128), f32)
    for k in range(3):
        tail = jnp.where(at == k, pooled[k], tail)
    meta = jnp.where(one < 64, reward, place.astype(f32))
    meta = jnp.broadcast_to(meta, (8, 128))
    for i in range(32):
        if i < half // 16:
            which = 0 if i < BW // 16 else 1
            acc = jnp.zeros((16, 128), f32)
            for s in range(NB):
                v = q_ref[s, i * 16 : (i + 1) * 16, :].astype(jnp.int32).astype(f32)
                acc = acc + v * (scale[s][which : which + 1] * (1.0 / STEPS))
        elif i == half // 16:
            acc = tail
        else:
            acc = jnp.zeros((16, 128), f32)
        out_ref[i, :16, :] = acc
        out_ref[i, 16:, :] = meta


def slope_kernel(info, d_ref, out_ref, loss_ref):
    told = d_ref[:, 16, :]
    lane = lanes((32, 128))
    row = lax.broadcasted_iota(jnp.int32, (32, 128), 0)
    r_col = jnp.sum(jnp.where(lane == 0, told, 0.0), axis=1, keepdims=True)
    k_col = jnp.sum(jnp.where(lane == 64, told, 0.0), axis=1, keepdims=True)
    r_row = jnp.sum(jnp.where(lane == row, r_col, 0.0), axis=0, keepdims=True)
    k_row = jnp.sum(jnp.where(lane == row, k_col, 0.0), axis=0, keepdims=True)
    real = lane < 32
    later = real & ((lane & 1) == (row & 1)) & (k_col >= k_row)
    top = jnp.max(jnp.where(later, r_col, -1e30), axis=0, keepdims=True)
    top = jnp.where(real[0:1], top, 0.0)
    ex = jnp.where(later, jnp.exp(jnp.where(later, r_col - top, 0.0)), 0.0)
    total = jnp.where(real[0:1], jnp.sum(ex, axis=0, keepdims=True), 1.0)
    slope = jnp.sum(ex / total, axis=1, keepdims=True) - 1.0
    terms = top + jnp.log(total) - r_row
    terms = jnp.where(real[0:1] & ((lane[0:1] & 1) == info[5]), terms, 0.0)
    loss_ref[...] = jnp.broadcast_to(jnp.sum(terms, axis=1, keepdims=True), (8, 128))
    acc = jnp.zeros((16, 128), f32)
    for i in range(32):
        acc = acc + d_ref[i, :16, :] * slope[i : i + 1]
    for i in range(32):
        out_ref[i] = acc


def on_device(hidden, lengths, starts, ranking, down_w, up_w, gain, head):
    x = hidden[0, 0]
    cand, fsdp, prompt = lax.axis_index("cand"), lax.axis_index("fsdp"), lax.axis_index("prompt")
    core = cand % 2
    gain_f, head_f = gain.astype(f32), head.astype(f32)
    both = gain_f * head_f
    near = lax.reduce_precision(both, 8, 7)
    hg_hi, hg_lo = near.astype(bf16), (both - near).astype(bf16)
    pad = jnp.zeros((BW, 128 - R), bf16)
    down_t = jnp.concatenate([down_w.T, hg_hi[:, None], hg_lo[:, None], pad[:, 2:]], axis=1)
    up_t = jnp.concatenate([up_w.T, pad], axis=1)
    slab = jnp.where(core == 0, down_t, up_t)
    mine = lax.all_to_all(jnp.broadcast_to(slab[None], (NB, BW, 128)), "fsdp", 0, 0, tiled=True)
    mine = mine.reshape(D, 128)
    other = lax.ppermute(mine, "cand", [(i, i ^ 1) for i in range(16)])
    info = jnp.stack([starts[0, 0], lengths[0, 0], fsdp * TOK, core, cand, prompt]).astype(jnp.int32)
    rows = BW + BW // 2 + 16
    coded_terms = pl.pallas_call(
        local_kernel,
        out_shape=jax.ShapeDtypeStruct((NB, rows, 128), jnp.int16),
        in_specs=[SMEM, VMEM, VMEM, VMEM],
        out_specs=VMEM,
        scratch_shapes=[
            pltpu.VMEM((D, 256), bf16),
            pltpu.VMEM((TOK, 1), f32),
            pltpu.VMEM((D, 256), f32),
            pltpu.VMEM((8, D + 256), f32),
        ],
        compiler_params=pltpu.CompilerParams(vmem_limit_bytes=48 << 20),
    )(info, x, mine, other)
    swapped = lax.all_to_all(coded_terms, "fsdp", 0, 0, tiled=True)
    sums = pl.pallas_call(
        block_kernel,
        out_shape=jax.ShapeDtypeStruct((32, 24, 128), f32),
        in_specs=[SMEM, SMEM, VMEM],
        out_specs=VMEM,
        compiler_params=pltpu.CompilerParams(vmem_limit_bytes=16 << 20),
    )(info, ranking, swapped)
    pieces = lax.all_to_all(sums, ("cand", "prompt"), 0, 0, tiled=True)
    share, loss = pl.pallas_call(
        slope_kernel,
        out_shape=(jax.ShapeDtypeStruct((32, 16, 128), f32), jax.ShapeDtypeStruct((8, 128), f32)),
        in_specs=[SMEM, VMEM],
        out_specs=(VMEM, VMEM),
        compiler_params=pltpu.CompilerParams(vmem_limit_bytes=16 << 20),
    )(info, pieces)
    final = lax.all_to_all(share, ("cand", "prompt"), 0, 0, tiled=True).reshape(512, 128)
    half = BW + BW // 2
    slab_a, slab_b = final[:BW], final[BW:half]
    pooled = final[half : half + 3].reshape(-1)[:BW]
    down_grad = slab_a[:, :R].T
    up_low = jnp.concatenate([slab_b[:, :64], slab_b[:, 64:]], axis=0)
    up_grad = jnp.concatenate([up_low, slab_a[:, R:]], axis=1).T
    return (loss[0, :1], down_grad, up_grad, head_f * pooled, gain_f * pooled)


def solution(mesh):
    placed = (
        P("prompt", "cand", "fsdp", None),
        P("prompt", "cand"),
        P("prompt", "cand"),
        P("prompt", None),
        P(None, "fsdp"),
        P(None, "fsdp"),
        P("fsdp"),
        P("fsdp"),
    )
    return jax.shard_map(
        on_device,
        mesh=mesh,
        in_specs=placed,
        out_specs=(P("prompt"), P(None, "fsdp"), P(None, "fsdp"), P("fsdp"), P("fsdp")),
        check_vma=False,
    )
```

```python
import jax
import jax.numpy as jnp
from jax import lax
from jax.experimental import pallas as pl
from jax.experimental.pallas import tpu as pltpu
from jax.sharding import PartitionSpec as P

loss_scale = 256.0
D = 4608
R = 96
TOK = 512
NB = 16
BW = 288
HALF = 2304
CH = 512
STEPS = 32760.0
FINE = 60000.0
TINY = 1e-36
f32 = jnp.float32
bf16 = jnp.bfloat16
VMEM = pl.BlockSpec(memory_space=pltpu.VMEM)
SMEM = pl.BlockSpec(memory_space=pltpu.SMEM)


def mm(a, b, ca, cb):
    return lax.dot_general(a, b, (((ca,), (cb,)), ((), ())), preferred_element_type=f32)


def halves(v):
    hi = v.astype(bf16)
    return hi, (v - hi.astype(f32)).astype(bf16)


def lanes(shape):
    return lax.broadcasted_iota(jnp.int32, shape, len(shape) - 1)


def level(most):
    return jnp.ceil(jnp.log2(jnp.maximum(most, TINY)) * 8.0)


def coded(v, e):
    return jnp.round(v * jnp.exp2(e * -0.125) * STEPS).astype(jnp.int32)


def pack_kernel(w_ref, out_ref):
    w = w_ref[...].astype(f32)
    w = jnp.concatenate([w, jnp.zeros((128, 96), f32)], axis=1)
    t = jnp.transpose(w)
    lane = lanes((64, 128))
    last = t[224:288]
    for i in range(3):
        cut = slice(64 * i, 64 * i + 64)
        rows = jnp.where(lane < R, t[cut], pltpu.roll(last, 96 - 32 * i, 1)).astype(bf16)
        for j in range(8):
            out_ref[j, cut, :] = rows
    lane = lanes((32, 128))
    rows = jnp.where(lane < R, t[192:224], 0.0)
    for k in range(9):
        piece = t[32 * k : 32 * k + 32]
        rows = jnp.where(lane == R + k, pltpu.roll(piece, k, 1) if k else piece, rows)
    rows = rows.astype(bf16)
    for j in range(8):
        out_ref[j, 192:, :] = rows


def unpack(q_ref, store):
    for j in range(8):
        q = q_ref[j].astype(f32)
        lane = lanes((32, 128))
        part = q[192:]
        cols = [pltpu.roll(part, 128 - k, 1) if k else part for k in range(9)]
        for k in range(7):
            rows = jnp.where(lane < R, q[32 * k : 32 * k + 32], jnp.where(lane == R, cols[k], 0.0))
            store(j * BW + 32 * k, rows.astype(bf16))
        for k in range(2):
            cut = [pltpu.roll(q[64 * i + 32 * k : 64 * i + 32 * k + 32], 32 * i + 32, 1) for i in range(3)]
            rows = jnp.where(lane < 32, cut[0], jnp.where(lane < 64, cut[1], cut[2]))
            rows = jnp.where(lane < R, rows, jnp.where(lane == R, cols[7 + k], 0.0))
            store(j * BW + 224 + 32 * k, rows.astype(bf16))


def unpack_both(core, mine_ref, other_ref, w_ref):
    def stores(left):
        def to_left(at, rows):
            w_ref[at : at + 32, :128] = rows

        def to_right(at, rows):
            w_ref[at : at + 32, 128:] = rows

        return (to_left, to_right) if left else (to_right, to_left)

    for left in (True, False):

        @pl.when((core == 0) == left)
        def _(left=left):
            first, second = stores(left)
            unpack(mine_ref, first)
            unpack(other_ref, second)


def near_kernel(x_ref, mine_ref, other_ref, w_ref, prod_ref, gram_ref, ss_ref):
    unpack_both(lax.axis_index("cand") % 2, mine_ref, other_ref, w_ref)

    def square(i, carry):
        at = pl.ds(pl.multiple_of(i * 16, 16), 16)
        rows = x_ref[at, :].astype(f32)
        ss_ref[at, :] = jnp.broadcast_to(jnp.sum(rows * rows, axis=1, keepdims=True), (16, 128))
        return carry

    lax.fori_loop(0, TOK // 16, square, 0)
    cols = pl.ds(pl.multiple_of(lax.axis_index("fsdp") // 8 * HALF, 128), HALF)
    prod_ref[...] = mm(x_ref[:, cols], w_ref[...], 1, 0)
    gram_ref[...] = mm(w_ref[...], w_ref[...], 0, 0)


def local_kernel(
    starts, lengths, x_ref, w_near, prod_near, gram_near, ss_ref, mine_ref, other_ref, out_ref, w_far, w_ref, g_ref, p_ref
):
    start, length = starts[0, 0], lengths[0, 0]
    first = lax.axis_index("fsdp") * TOK
    core = lax.axis_index("cand") % 2
    side = lax.axis_index("fsdp") // 8
    unpack_both(core, mine_ref, other_ref, w_far)
    w_ref[pl.ds(pl.multiple_of(side * HALF, 256), HALF), :] = w_near[...]
    w_ref[pl.ds(pl.multiple_of((1 - side) * HALF, 256), HALF), :] = w_far[...]
    cols = pl.ds(pl.multiple_of((1 - side) * HALF, 128), HALF)
    prod = prod_near[...] + mm(x_ref[:, cols], w_far[...], 1, 0)
    gram = gram_near[...] + mm(w_far[...], w_far[...], 0, 0)
    pre = prod[:, :128]
    x_up = prod[:, 128:]
    lane = lanes((TOK, 128))
    unit = lane < R
    sig = 1.0 / (1.0 + jnp.exp(-pre))
    act_b = jnp.where(unit, pre * sig, 0.0).astype(bf16)
    act = act_b.astype(f32)
    g_hi, g_lo = halves(gram[128:, :])
    through = mm(act_b, g_hi, 1, 0) + mm(act_b, g_lo, 1, 0)
    m_left = pre + through[:, :128]
    m_up = x_up + through[:, 128:]
    m_head = jnp.sum(jnp.where(lane == R, m_left + m_up, 0.0), axis=1, keepdims=True)
    m_sq = ss_ref[:, :1] + jnp.sum(act * (x_up + m_up), axis=1, keepdims=True)
    inv = lax.rsqrt(jnp.maximum(m_sq, 0.0) * (1.0 / D) + 1e-06)
    score = inv * m_head
    count = (length - start).astype(f32)
    pos = first + lax.broadcasted_iota(jnp.int32, (TOK, 1), 0)
    valid = (pos >= start) & (pos < length)
    part = jnp.sum(jnp.where(valid, score, 0.0), axis=0, keepdims=True) / count
    weight = jnp.where(valid, loss_scale / count, 0.0)
    alpha = inv * weight
    beta = inv * inv * weight * score * (1.0 / D)
    up_head = gram[R : R + 1, 128:] + gram[128 + R : 129 + R, 128:]
    back = alpha * up_head - beta * m_up
    pre_grad = back * sig * (1.0 + pre * (1.0 - sig))
    nab = -(act * beta)
    left = jnp.where(unit, pre_grad, pltpu.roll(nab, 32, 1))
    right = jnp.where(lane < 64, nab, pltpu.roll(nab, 64, 1))
    lhs = jnp.concatenate([left, right], axis=1).astype(bf16)
    a_left = jnp.where(unit, 0.0, pltpu.roll(act, 32, 1))
    a_right = jnp.where(lane < 64, act, pltpu.roll(act, 64, 1))
    u_row = jnp.sum(alpha * jnp.concatenate([a_left, a_right], axis=1), axis=0, keepdims=True)
    v_row = jnp.sum(alpha * act, axis=0, keepdims=True)
    low = mm(act_b, lhs, 0, 0)
    low = jnp.where(lanes((128, 256)) < R, 0.0, low)
    row = lax.broadcasted_iota(jnp.int32, (128, 256), 0)
    top = jnp.where(row == R, u_row, 0.0)
    low = jnp.where(row == R, u_row, low)
    c_hi, c_lo = halves(jnp.concatenate([top, low], axis=0))
    for i in range(D // CH):
        cut = slice(i * CH, (i + 1) * CH)
        w = w_ref[cut, :]
        g_ref[cut, :] = mm(x_ref[:, cut], lhs, 0, 0) + (mm(w, c_hi, 1, 0) + mm(w, c_lo, 1, 0))

    al_hi = alpha.astype(bf16).astype(f32)
    al_lo = alpha - al_hi
    al = jnp.where(lane == 0, al_hi, jnp.where(lane == 1, al_lo, 0.0))
    al = jnp.transpose(al)[:16].astype(bf16)
    v_hi = v_row.astype(bf16).astype(f32)
    row = lax.broadcasted_iota(jnp.int32, (16, 128), 0)
    vv = jnp.where(row == 0, v_hi, jnp.where(row == 1, v_row - v_hi, 0.0)).astype(bf16)
    pooled = mm(al, x_ref[...], 1, 0) + mm(vv, w_ref[:, 128:], 1, 1)
    p_ref[:, D:] = jnp.zeros((8, 256), f32)
    p_ref[:, :D] = jnp.broadcast_to(pooled[0:1] + pooled[1:2], (8, D))

    s_e = level(jnp.abs(part))
    s_v = part * jnp.exp2(s_e * -0.125) * STEPS
    s_hi = jnp.round(s_v)
    s_lo = jnp.round((s_v - s_hi) * FINE)
    one = lanes((1, 128))
    s_row = jnp.where(one == 0, s_e, jnp.where(one == 1, s_hi, jnp.where(one == 2, s_lo, 0.0))).astype(jnp.int32)
    for j in range(NB):
        a = g_ref[j * BW : (j + 1) * BW, :128]
        b0 = g_ref[j * BW : j * BW + BW // 2, 128:]
        b1 = g_ref[j * BW + BW // 2 : (j + 1) * BW, 128:]
        b = jnp.where(lanes((BW // 2, 128)) < 64, b0, b1)
        a_e = level(jnp.max(jnp.abs(a), axis=0, keepdims=True))
        b_e = level(jnp.max(jnp.abs(b), axis=0, keepdims=True))
        out_ref[j, :BW, :] = coded(a, a_e).astype(jnp.int16)
        out_ref[j, BW : BW + BW // 2, :] = coded(b, b_e).astype(jnp.int16)
        base = j * BW // 128 * 128
        window = p_ref[:, base : base + 512]
        off = j * BW - base
        if off:
            window = pltpu.roll(window, 512 - off, 1)
        window = jnp.where(lanes((8, 512)) < BW, window, 0.0)
        p_e = level(jnp.max(jnp.abs(window), axis=1, keepdims=True))
        p_q = coded(window, p_e)
        at = lax.broadcasted_iota(jnp.int32, (16, 128), 0)
        rows = (
            a_e.astype(jnp.int32),
            b_e.astype(jnp.int32),
            p_q[0:1, :128],
            p_q[0:1, 128:256],
            p_q[0:1, 256:384],
            jnp.broadcast_to(p_e[0:1].astype(jnp.int32), (1, 128)),
            s_row,
        )
        meta = jnp.zeros((16, 128), jnp.int32)
        for k, r in enumerate(rows):
            meta = jnp.where(at == k, r, meta)
        out_ref[j, BW + BW // 2 :, :] = meta.astype(jnp.int16)


def block_kernel(ranking, q_ref, out_ref):
    mine = lax.axis_index("cand")
    place = jnp.int32(0)
    for k in range(16):
        place = jnp.where(ranking[0, k] == mine, jnp.int32(k), place)
    half = BW + BW // 2
    parts = [q_ref[s, half:, :].astype(jnp.int32).astype(f32) for s in range(NB)]
    scale = [jnp.exp2(m * 0.125) for m in parts]
    pooled = [jnp.zeros((1, 128), f32) for _ in range(3)]
    reward = jnp.zeros((1, 128), f32)
    one = lanes((1, 128))
    for s in range(NB):
        m, e = parts[s], scale[s] * (1.0 / STEPS)
        for k in range(3):
            pooled[k] = pooled[k] + m[2 + k : 3 + k] * e[5:6]
        told = jnp.where(one == 1, m[6:7], jnp.where(one == 2, m[6:7] * (1.0 / FINE), 0.0))
        told = jnp.sum(told, axis=1, keepdims=True)
        by = jnp.sum(jnp.where(one == 0, e[6:7], 0.0), axis=1, keepdims=True)
        reward = reward + told * by
    at = lax.broadcasted_iota(jnp.int32, (16, 128), 0)
    tail = jnp.zeros((16, 128), f32)
    for k in range(3):
        tail = jnp.where(at == k, pooled[k], tail)
    meta = jnp.where(one < 64, reward, place.astype(f32))
    meta = jnp.broadcast_to(meta, (8, 128))
    for i in range(28):
        if i < half // 16:
            which = 0 if i < BW // 16 else 1
            acc = jnp.zeros((16, 128), f32)
            for s in range(NB):
                v = q_ref[s, i * 16 : (i + 1) * 16, :].astype(jnp.int32).astype(f32)
                acc = acc + v * (scale[s][which : which + 1] * (1.0 / STEPS))
        else:
            acc = tail
        for g in (2 * i, 2 * i + 1):
            at = g % 7 * 8
            out_ref[g // 7, at : at + 8, :] = acc[g % 2 * 8 : g % 2 * 8 + 8]
    for i in range(8):
        out_ref[i, 56:, :] = meta


def slope_kernel(d_ref, o_ref, out_ref, loss_ref):
    told = jnp.concatenate([d_ref[:, 56, :], o_ref[:, 56, :]], axis=0)
    lane = lanes((16, 128))
    row = lax.broadcasted_iota(jnp.int32, (16, 128), 0)
    r_col = jnp.sum(jnp.where(lane == 0, told, 0.0), axis=1, keepdims=True)
    k_col = jnp.sum(jnp.where(lane == 64, told, 0.0), axis=1, keepdims=True)
    r_row = jnp.sum(jnp.where(lane == row, r_col, 0.0), axis=0, keepdims=True)
    k_row = jnp.sum(jnp.where(lane == row, k_col, 0.0), axis=0, keepdims=True)
    real = lane < 16
    later = real & (k_col >= k_row)
    top = jnp.max(jnp.where(later, r_col, -1e30), axis=0, keepdims=True)
    top = jnp.where(real[0:1], top, 0.0)
    ex = jnp.where(later, jnp.exp(jnp.where(later, r_col - top, 0.0)), 0.0)
    total = jnp.where(real[0:1], jnp.sum(ex, axis=0, keepdims=True), 1.0)
    slope = jnp.sum(ex / total, axis=1, keepdims=True) - 1.0
    terms = jnp.where(real[0:1], top + jnp.log(total) - r_row, 0.0)
    loss_ref[...] = jnp.broadcast_to(jnp.sum(terms, axis=1, keepdims=True), (8, 128))
    acc = jnp.zeros((56, 128), f32)
    for i in range(8):
        acc = acc + d_ref[i, :56, :] * slope[i : i + 1] + o_ref[i, :56, :] * slope[8 + i : 9 + i]
    out_ref[...] = acc


def on_device(hidden, lengths, starts, ranking, down_w, up_w, gain, head):
    x = hidden[0, 0]
    core = lax.axis_index("cand") % 2
    sibling = [(i, i ^ 1) for i in range(16)]
    both = gain.astype(f32) * head.astype(f32)
    near = lax.reduce_precision(both, 8, 7)
    part = jnp.where(core == 0, near, both - near).astype(bf16)
    half_w = jnp.where(core == 0, down_w, up_w)
    half_w = jnp.concatenate([half_w, jnp.broadcast_to(part[None], (32, BW))], axis=0)
    packed = pl.pallas_call(
        pack_kernel,
        out_shape=jax.ShapeDtypeStruct((8, 224, 128), bf16),
        in_specs=[VMEM],
        out_specs=VMEM,
        compiler_params=pltpu.CompilerParams(vmem_limit_bytes=16 << 20),
    )(half_w)
    along_y = [list(range(8)), list(range(8, 16))]
    mine = lax.all_to_all(packed, "fsdp", 0, 0, axis_index_groups=along_y, tiled=True)
    across = [(i, i ^ 8) for i in range(16)]
    far_mine = lax.ppermute(mine, "fsdp", across)
    other = lax.ppermute(mine, "cand", sibling)
    w_near, prod, gram, squares = pl.pallas_call(
        near_kernel,
        out_shape=(
            jax.ShapeDtypeStruct((HALF, 256), bf16),
            jax.ShapeDtypeStruct((TOK, 256), f32),
            jax.ShapeDtypeStruct((256, 256), f32),
            jax.ShapeDtypeStruct((TOK, 128), f32),
        ),
        in_specs=[VMEM, VMEM, VMEM],
        out_specs=(VMEM, VMEM, VMEM, VMEM),
        compiler_params=pltpu.CompilerParams(vmem_limit_bytes=24 << 20),
    )(x, mine, other)
    far_mine, squares = lax.optimization_barrier((far_mine, squares))
    far_other = lax.ppermute(far_mine, "cand", sibling)
    rows = BW + BW // 2 + 16
    coded_terms = pl.pallas_call(
        local_kernel,
        out_shape=jax.ShapeDtypeStruct((NB, rows, 128), jnp.int16),
        in_specs=[SMEM, SMEM] + [VMEM] * 7,
        out_specs=VMEM,
        scratch_shapes=[
            pltpu.VMEM((HALF, 256), bf16),
            pltpu.VMEM((D, 256), bf16),
            pltpu.VMEM((D, 256), f32),
            pltpu.VMEM((8, D + 256), f32),
        ],
        compiler_params=pltpu.CompilerParams(vmem_limit_bytes=40 << 20),
    )(starts, lengths, x, w_near, prod, gram, squares, far_mine, far_other)
    swapped = lax.all_to_all(coded_terms, "fsdp", 0, 0, tiled=True)
    sums = pl.pallas_call(
        block_kernel,
        out_shape=jax.ShapeDtypeStruct((8, 64, 128), f32),
        in_specs=[SMEM, VMEM],
        out_specs=VMEM,
        compiler_params=pltpu.CompilerParams(vmem_limit_bytes=16 << 20),
    )(ranking, swapped)
    along_z = [list(range(0, 16, 2)), list(range(1, 16, 2))]
    pieces = lax.all_to_all(sums, "cand", 0, 0, axis_index_groups=along_z, tiled=True)
    beside = lax.ppermute(pieces, "cand", sibling)
    share, loss = pl.pallas_call(
        slope_kernel,
        out_shape=(jax.ShapeDtypeStruct((56, 128), f32), jax.ShapeDtypeStruct((8, 128), f32)),
        in_specs=[VMEM, VMEM],
        out_specs=(VMEM, VMEM),
        compiler_params=pltpu.CompilerParams(vmem_limit_bytes=16 << 20),
    )(pieces, beside)
    share = share + lax.ppermute(share, "prompt", [(0, 1), (1, 0)])
    final = jnp.broadcast_to(share[None], (8, 56, 128))
    final = lax.all_to_all(final, "cand", 0, 0, axis_index_groups=along_z, tiled=True).reshape(448, 128)
    half = BW + BW // 2
    slab_a, slab_b = final[:BW], final[BW:half]
    pooled = final[half : half + 3].reshape(-1)[:BW]
    down_grad = slab_a[:, :R].T
    up_low = jnp.concatenate([slab_b[:, :64], slab_b[:, 64:]], axis=0)
    up_grad = jnp.concatenate([up_low, slab_a[:, R:]], axis=1).T
    gain_f, head_f = gain.astype(f32), head.astype(f32)
    return (loss[0, :1], down_grad, up_grad, head_f * pooled, gain_f * pooled)


def solution(mesh):
    placed = (
        P("prompt", "cand", "fsdp", None),
        P("prompt", "cand"),
        P("prompt", "cand"),
        P("prompt", None),
        P(None, "fsdp"),
        P(None, "fsdp"),
        P("fsdp"),
        P("fsdp"),
    )
    return jax.shard_map(
        on_device,
        mesh=mesh,
        in_specs=placed,
        out_specs=(P("prompt"), P(None, "fsdp"), P(None, "fsdp"), P("fsdp"), P("fsdp")),
        check_vma=False,
    )
```

```python
import jax
import jax.numpy as jnp
from jax import lax
from jax.experimental import pallas as pl
from jax.experimental.pallas import tpu as pltpu
from jax.sharding import PartitionSpec as P

loss_scale = 256.0
D = 4608
R = 96
TOK = 512
NB = 16
BW = 288
HALF = 2304
CH = 512
CUT = 224
STEPS = 32760.0
FINE = 60000.0
TINY = 1e-36
f32 = jnp.float32
bf16 = jnp.bfloat16
VMEM = pl.BlockSpec(memory_space=pltpu.VMEM)
SMEM = pl.BlockSpec(memory_space=pltpu.SMEM)


def mm(a, b, ca, cb):
    return lax.dot_general(a, b, (((ca,), (cb,)), ((), ())), preferred_element_type=f32)


def halves(v):
    hi = v.astype(bf16)
    return hi, (v - hi.astype(f32)).astype(bf16)


def lanes(shape):
    return lax.broadcasted_iota(jnp.int32, shape, len(shape) - 1)


def level(most):
    return jnp.ceil(jnp.log2(jnp.maximum(most, TINY)) * 8.0)


def coded(v, e):
    return jnp.round(v * jnp.exp2(e * -0.125) * STEPS).astype(jnp.int32)


def told_row(part):
    e = level(jnp.abs(part))
    v = part * jnp.exp2(e * -0.125) * STEPS
    hi = jnp.round(v)
    lo = jnp.round((v - hi) * FINE)
    one = lanes((1, 128))
    return jnp.where(one == 0, e, jnp.where(one == 1, hi, jnp.where(one == 2, lo, 0.0))).astype(jnp.int32)


def told(m, scale):
    one = lanes((1, 128))
    v = jnp.where(one == 1, m[6:7], jnp.where(one == 2, m[6:7] * (1.0 / FINE), 0.0))
    by = jnp.sum(jnp.where(one == 0, scale[6:7], 0.0), axis=1, keepdims=True)
    return jnp.sum(v, axis=1, keepdims=True) * (by * (1.0 / STEPS))


def meta_rows(a_e, b_e, window, s_row):
    p_e = level(jnp.max(jnp.abs(window), axis=1, keepdims=True))
    p_q = coded(window, p_e)
    rows = (
        a_e.astype(jnp.int32),
        b_e.astype(jnp.int32),
        p_q[0:1, :128],
        p_q[0:1, 128:256],
        p_q[0:1, 256:384],
        jnp.broadcast_to(p_e[0:1].astype(jnp.int32), (1, 128)),
        s_row,
    )
    at = lax.broadcasted_iota(jnp.int32, (16, 128), 0)
    meta = jnp.zeros((16, 128), jnp.int32)
    for k, r in enumerate(rows):
        meta = jnp.where(at == k, r, meta)
    return meta.astype(jnp.int16)


def pack_kernel(w_ref, out_ref):
    w = w_ref[...].astype(f32)
    w = jnp.concatenate([w, jnp.zeros((128, 96), f32)], axis=1)
    t = jnp.transpose(w)
    lane = lanes((64, 128))
    last = t[224:288]
    for i in range(3):
        cut = slice(64 * i, 64 * i + 64)
        rows = jnp.where(lane < R, t[cut], pltpu.roll(last, 96 - 32 * i, 1)).astype(bf16)
        for j in range(8):
            out_ref[j, cut, :] = rows
    lane = lanes((32, 128))
    rows = jnp.where(lane < R, t[192:224], 0.0)
    for k in range(9):
        piece = t[32 * k : 32 * k + 32]
        rows = jnp.where(lane == R + k, pltpu.roll(piece, k, 1) if k else piece, rows)
    rows = rows.astype(bf16)
    for j in range(8):
        out_ref[j, 192:, :] = rows


def unpack(q_ref, store):
    for j in range(8):
        q = q_ref[j].astype(f32)
        lane = lanes((32, 128))
        part = q[192:]
        cols = [pltpu.roll(part, 128 - k, 1) if k else part for k in range(9)]
        for k in range(7):
            rows = jnp.where(lane < R, q[32 * k : 32 * k + 32], jnp.where(lane == R, cols[k], 0.0))
            store(j * BW + 32 * k, rows.astype(bf16))
        for k in range(2):
            cut = [pltpu.roll(q[64 * i + 32 * k : 64 * i + 32 * k + 32], 32 * i + 32, 1) for i in range(3)]
            rows = jnp.where(lane < 32, cut[0], jnp.where(lane < 64, cut[1], cut[2]))
            rows = jnp.where(lane < R, rows, jnp.where(lane == R, cols[7 + k], 0.0))
            store(j * BW + 224 + 32 * k, rows.astype(bf16))


def unpack_both(core, mine_ref, other_ref, w_ref):
    def stores(left):
        def to_left(at, rows):
            w_ref[at : at + 32, :128] = rows

        def to_right(at, rows):
            w_ref[at : at + 32, 128:] = rows

        return (to_left, to_right) if left else (to_right, to_left)

    for left in (True, False):

        @pl.when((core == 0) == left)
        def _(left=left):
            first, second = stores(left)
            unpack(mine_ref, first)
            unpack(other_ref, second)


def near_kernel(x_ref, mine_ref, other_ref, w_ref, prod_ref, gram_ref, ss_ref):
    unpack_both(lax.axis_index("cand") % 2, mine_ref, other_ref, w_ref)

    def square(i, carry):
        at = pl.ds(pl.multiple_of(i * 16, 16), 16)
        rows = x_ref[at, :].astype(f32)
        ss_ref[at, :] = jnp.broadcast_to(jnp.sum(rows * rows, axis=1, keepdims=True), (16, 128))
        return carry

    lax.fori_loop(0, TOK // 16, square, 0)
    cols = pl.ds(pl.multiple_of(lax.axis_index("fsdp") // 8 * HALF, 128), HALF)
    prod_ref[...] = mm(x_ref[:, cols], w_ref[...], 1, 0)
    gram_ref[...] = mm(w_ref[...], w_ref[...], 0, 0)


def local_kernel(
    starts,
    lengths,
    x_ref,
    w_near,
    prod_near,
    gram_near,
    ss_ref,
    mine_ref,
    other_ref,
    send_a,
    send_b,
    own_a,
    own_b,
    own_p,
    own_s,
    w_far,
    w_ref,
    g_ref,
    p_ref,
):
    start, length = starts[0, 0], lengths[0, 0]
    first = lax.axis_index("fsdp") * TOK
    core = lax.axis_index("cand") % 2
    side = lax.axis_index("fsdp") // 8
    unpack_both(core, mine_ref, other_ref, w_far)
    w_ref[pl.ds(pl.multiple_of(side * HALF, 256), HALF), :] = w_near[...]
    w_ref[pl.ds(pl.multiple_of((1 - side) * HALF, 256), HALF), :] = w_far[...]
    cols = pl.ds(pl.multiple_of((1 - side) * HALF, 128), HALF)
    prod = prod_near[...] + mm(x_ref[:, cols], w_far[...], 1, 0)
    gram = gram_near[...] + mm(w_far[...], w_far[...], 0, 0)
    pre = prod[:, :128]
    x_up = prod[:, 128:]
    lane = lanes((TOK, 128))
    unit = lane < R
    sig = 1.0 / (1.0 + jnp.exp(-pre))
    act_b = jnp.where(unit, pre * sig, 0.0).astype(bf16)
    act = act_b.astype(f32)
    g_hi, g_lo = halves(gram[128:, :])
    through = mm(act_b, g_hi, 1, 0) + mm(act_b, g_lo, 1, 0)
    m_left = pre + through[:, :128]
    m_up = x_up + through[:, 128:]
    m_head = jnp.sum(jnp.where(lane == R, m_left + m_up, 0.0), axis=1, keepdims=True)
    m_sq = ss_ref[:, :1] + jnp.sum(act * (x_up + m_up), axis=1, keepdims=True)
    inv = lax.rsqrt(jnp.maximum(m_sq, 0.0) * (1.0 / D) + 1e-06)
    score = inv * m_head
    count = (length - start).astype(f32)
    pos = first + lax.broadcasted_iota(jnp.int32, (TOK, 1), 0)
    valid = (pos >= start) & (pos < length)
    part = jnp.sum(jnp.where(valid, score, 0.0), axis=0, keepdims=True) / count
    weight = jnp.where(valid, loss_scale / count, 0.0)
    alpha = inv * weight
    beta = inv * inv * weight * score * (1.0 / D)
    up_head = gram[R : R + 1, 128:] + gram[128 + R : 129 + R, 128:]
    back = alpha * up_head - beta * m_up
    pre_grad = back * sig * (1.0 + pre * (1.0 - sig))
    nab = -(act * beta)
    left = jnp.where(unit, pre_grad, pltpu.roll(nab, 32, 1))
    right = jnp.where(lane < 64, nab, pltpu.roll(nab, 64, 1))
    lhs = jnp.concatenate([left, right], axis=1).astype(bf16)
    a_left = jnp.where(unit, 0.0, pltpu.roll(act, 32, 1))
    a_right = jnp.where(lane < 64, act, pltpu.roll(act, 64, 1))
    u_row = jnp.sum(alpha * jnp.concatenate([a_left, a_right], axis=1), axis=0, keepdims=True)
    v_row = jnp.sum(alpha * act, axis=0, keepdims=True)
    low = mm(act_b, lhs, 0, 0)
    low = jnp.where(lanes((128, 256)) < R, 0.0, low)
    row = lax.broadcasted_iota(jnp.int32, (128, 256), 0)
    top = jnp.where(row == R, u_row, 0.0)
    low = jnp.where(row == R, u_row, low)
    c_hi, c_lo = halves(jnp.concatenate([top, low], axis=0))
    for i in range(D // CH):
        cut = slice(i * CH, (i + 1) * CH)
        w = w_ref[cut, :]
        g_ref[cut, :] = mm(x_ref[:, cut], lhs, 0, 0) + (mm(w, c_hi, 1, 0) + mm(w, c_lo, 1, 0))

    al_hi = alpha.astype(bf16).astype(f32)
    al_lo = alpha - al_hi
    al = jnp.where(lane == 0, al_hi, jnp.where(lane == 1, al_lo, 0.0))
    al = jnp.transpose(al)[:16].astype(bf16)
    v_hi = v_row.astype(bf16).astype(f32)
    row = lax.broadcasted_iota(jnp.int32, (16, 128), 0)
    vv = jnp.where(row == 0, v_hi, jnp.where(row == 1, v_row - v_hi, 0.0)).astype(bf16)
    pooled = mm(al, x_ref[...], 1, 0) + mm(vv, w_ref[:, 128:], 1, 1)
    p_ref[:, D:] = jnp.zeros((8, 256), f32)
    p_ref[:, :D] = jnp.broadcast_to(pooled[0:1] + pooled[1:2], (8, D))

    def window(j):
        base = j * BW // 128 * 128
        off = j * BW - base
        w = p_ref[:, base : base + 512]
        if off:
            w = pltpu.roll(w, 512 - off, 1)
        return jnp.where(lanes((8, 512)) < BW, w, 0.0)

    def block(j):
        a = g_ref[pl.ds(pl.multiple_of(j * BW, 32), BW), :128]
        b0 = g_ref[pl.ds(pl.multiple_of(j * BW, 32), BW // 2), 128:]
        b1 = g_ref[pl.ds(pl.multiple_of(j * BW + BW // 2, 16), BW // 2), 128:]
        return a, jnp.where(lanes((BW // 2, 128)) < 64, b0, b1)

    par = lax.axis_index("fsdp") % 2
    s_row = told_row(part)
    own_s[...] = jnp.broadcast_to(part, (8, 128))
    for i in range(8):
        even, odd = window(2 * i), window(2 * i + 1)
        a, b = block(2 * i + 1 - par)
        a_e = level(jnp.max(jnp.abs(a), axis=0, keepdims=True))
        b_e = level(jnp.max(jnp.abs(b), axis=0, keepdims=True))
        q = coded(a, a_e).astype(jnp.int16)
        meta = meta_rows(a_e, b_e, jnp.where(par == 0, odd, even), s_row)
        send_a[i, :CUT, :] = q[:CUT]
        send_a[i, CUT:, :] = meta
        send_b[i, : BW - CUT, :] = q[CUT:]
        send_b[i, BW - CUT : BW - CUT + BW // 2, :] = coded(b, b_e).astype(jnp.int16)
        send_b[i, BW - CUT + BW // 2 :, :] = meta
        a, b = block(2 * i + par)
        own_a[i] = a
        own_b[i] = b
        own_p[i] = jnp.where(par == 0, even, odd)


def pair_kernel(got_a, got_b, own_a, own_b, own_p, own_s, out_ref):
    end = BW - CUT + BW // 2
    m_a = [got_a[i, CUT:, :].astype(jnp.int32).astype(f32) for i in range(8)]
    m_b = [got_b[i, end:, :].astype(jnp.int32).astype(f32) for i in range(8)]
    scale = jnp.exp2(m_b[0] * 0.125)
    s_row = told_row(own_s[0:1, 0:1] + told(m_b[0], scale))
    for i in range(8):
        by_a = jnp.exp2(m_a[i][0:1] * 0.125) * (1.0 / STEPS)
        by = jnp.exp2(m_b[i] * 0.125) * (1.0 / STEPS)
        top = own_a[i, :CUT] + got_a[i, :CUT, :].astype(jnp.int32).astype(f32) * by_a
        low = own_a[i, CUT:] + got_b[i, : BW - CUT, :].astype(jnp.int32).astype(f32) * by[0:1]
        b = own_b[i] + got_b[i, BW - CUT : end, :].astype(jnp.int32).astype(f32) * by[1:2]
        m = m_b[i]
        got_p = jnp.concatenate([m[2:3], m[3:4], m[4:5], jnp.zeros((1, 128), f32)], axis=1)
        p = own_p[i] + got_p * jnp.concatenate([by[5:6]] * 4, axis=1)
        most = jnp.maximum(
            jnp.max(jnp.abs(top), axis=0, keepdims=True), jnp.max(jnp.abs(low), axis=0, keepdims=True)
        )
        a_e = level(most)
        b_e = level(jnp.max(jnp.abs(b), axis=0, keepdims=True))
        out_ref[i, :CUT, :] = coded(top, a_e).astype(jnp.int16)
        out_ref[i, CUT:BW, :] = coded(low, a_e).astype(jnp.int16)
        out_ref[i, BW : BW + BW // 2, :] = coded(b, b_e).astype(jnp.int16)
        out_ref[i, BW + BW // 2 :, :] = meta_rows(a_e, b_e, p, s_row)


def block_kernel(ranking, q_ref, out_ref):
    mine = lax.axis_index("cand")
    place = jnp.int32(0)
    for k in range(16):
        place = jnp.where(ranking[0, k] == mine, jnp.int32(k), place)
    half = BW + BW // 2
    parts = [q_ref[s, half:, :].astype(jnp.int32).astype(f32) for s in range(8)]
    scale = [jnp.exp2(m * 0.125) for m in parts]
    pooled = [jnp.zeros((1, 128), f32) for _ in range(3)]
    reward = jnp.zeros((1, 1), f32)
    one = lanes((1, 128))
    for s in range(8):
        m, e = parts[s], scale[s] * (1.0 / STEPS)
        for k in range(3):
            pooled[k] = pooled[k] + m[2 + k : 3 + k] * e[5:6]
        reward = reward + told(m, scale[s])
    at = lax.broadcasted_iota(jnp.int32, (16, 128), 0)
    tail = jnp.zeros((16, 128), f32)
    for k in range(3):
        tail = jnp.where(at == k, pooled[k], tail)
    meta = jnp.where(one < 64, reward, place.astype(f32))
    meta = jnp.broadcast_to(meta, (8, 128))
    for i in range(28):
        if i < half // 16:
            which = 0 if i < BW // 16 else 1
            acc = jnp.zeros((16, 128), f32)
            for s in range(8):
                v = q_ref[s, i * 16 : (i + 1) * 16, :].astype(jnp.int32).astype(f32)
                acc = acc + v * (scale[s][which : which + 1] * (1.0 / STEPS))
        else:
            acc = tail
        for g in (2 * i, 2 * i + 1):
            at = g % 7 * 8
            out_ref[g // 7, at : at + 8, :] = acc[g % 2 * 8 : g % 2 * 8 + 8]
    for i in range(8):
        out_ref[i, 56:, :] = meta


def slope_kernel(d_ref, o_ref, out_ref, loss_ref):
    told = jnp.concatenate([d_ref[:, 56, :], o_ref[:, 56, :]], axis=0)
    lane = lanes((16, 128))
    row = lax.broadcasted_iota(jnp.int32, (16, 128), 0)
    r_col = jnp.sum(jnp.where(lane == 0, told, 0.0), axis=1, keepdims=True)
    k_col = jnp.sum(jnp.where(lane == 64, told, 0.0), axis=1, keepdims=True)
    r_row = jnp.sum(jnp.where(lane == row, r_col, 0.0), axis=0, keepdims=True)
    k_row = jnp.sum(jnp.where(lane == row, k_col, 0.0), axis=0, keepdims=True)
    real = lane < 16
    later = real & (k_col >= k_row)
    top = jnp.max(jnp.where(later, r_col, -1e30), axis=0, keepdims=True)
    top = jnp.where(real[0:1], top, 0.0)
    ex = jnp.where(later, jnp.exp(jnp.where(later, r_col - top, 0.0)), 0.0)
    total = jnp.where(real[0:1], jnp.sum(ex, axis=0, keepdims=True), 1.0)
    slope = jnp.sum(ex / total, axis=1, keepdims=True) - 1.0
    terms = jnp.where(real[0:1], top + jnp.log(total) - r_row, 0.0)
    loss_ref[...] = jnp.broadcast_to(jnp.sum(terms, axis=1, keepdims=True), (8, 128))
    acc = jnp.zeros((56, 128), f32)
    for i in range(8):
        acc = acc + d_ref[i, :56, :] * slope[i : i + 1] + o_ref[i, :56, :] * slope[8 + i : 9 + i]
    out_ref[...] = acc


def on_device(hidden, lengths, starts, ranking, down_w, up_w, gain, head):
    x = hidden[0, 0]
    core = lax.axis_index("cand") % 2
    sibling = [(i, i ^ 1) for i in range(16)]
    both = gain.astype(f32) * head.astype(f32)
    near = lax.reduce_precision(both, 8, 7)
    part = jnp.where(core == 0, near, both - near).astype(bf16)
    half_w = jnp.where(core == 0, down_w, up_w)
    half_w = jnp.concatenate([half_w, jnp.broadcast_to(part[None], (32, BW))], axis=0)
    packed = pl.pallas_call(
        pack_kernel,
        out_shape=jax.ShapeDtypeStruct((8, 224, 128), bf16),
        in_specs=[VMEM],
        out_specs=VMEM,
        compiler_params=pltpu.CompilerParams(vmem_limit_bytes=16 << 20),
    )(half_w)
    along_y = [list(range(8)), list(range(8, 16))]
    mine = lax.all_to_all(packed, "fsdp", 0, 0, axis_index_groups=along_y, tiled=True)
    across = [(i, i ^ 8) for i in range(16)]
    far_mine = lax.ppermute(mine, "fsdp", across)
    other = lax.ppermute(mine, "cand", sibling)
    w_near, prod, gram, squares = pl.pallas_call(
        near_kernel,
        out_shape=(
            jax.ShapeDtypeStruct((HALF, 256), bf16),
            jax.ShapeDtypeStruct((TOK, 256), f32),
            jax.ShapeDtypeStruct((256, 256), f32),
            jax.ShapeDtypeStruct((TOK, 128), f32),
        ),
        in_specs=[VMEM, VMEM, VMEM],
        out_specs=(VMEM, VMEM, VMEM, VMEM),
        compiler_params=pltpu.CompilerParams(vmem_limit_bytes=24 << 20),
    )(x, mine, other)
    far_mine, squares = lax.optimization_barrier((far_mine, squares))
    far_other = lax.ppermute(far_mine, "cand", sibling)
    rows = BW + BW // 2 + 16
    send_a, send_b, *own = pl.pallas_call(
        local_kernel,
        out_shape=(
            jax.ShapeDtypeStruct((8, CUT + 16, 128), jnp.int16),
            jax.ShapeDtypeStruct((8, rows - CUT, 128), jnp.int16),
            jax.ShapeDtypeStruct((8, BW, 128), f32),
            jax.ShapeDtypeStruct((8, BW // 2, 128), f32),
            jax.ShapeDtypeStruct((8, 8, 512), f32),
            jax.ShapeDtypeStruct((8, 128), f32),
        ),
        in_specs=[SMEM, SMEM] + [VMEM] * 7,
        out_specs=(VMEM,) * 6,
        scratch_shapes=[
            pltpu.VMEM((HALF, 256), bf16),
            pltpu.VMEM((D, 256), bf16),
            pltpu.VMEM((D, 256), f32),
            pltpu.VMEM((8, D + 256), f32),
        ],
        compiler_params=pltpu.CompilerParams(vmem_limit_bytes=40 << 20),
    )(starts, lengths, x, w_near, prod, gram, squares, far_mine, far_other)
    got_a = lax.ppermute(send_a, "fsdp", [(i, i ^ 1) for i in range(16)])
    turn = [(i, i // 8 * 8 + (i + (1 if i % 2 else 7)) % 8) for i in range(16)]
    got_b = lax.ppermute(send_b, "fsdp", turn)
    coded_terms = pl.pallas_call(
        pair_kernel,
        out_shape=jax.ShapeDtypeStruct((8, rows, 128), jnp.int16),
        in_specs=[VMEM] * 6,
        out_specs=VMEM,
        compiler_params=pltpu.CompilerParams(vmem_limit_bytes=24 << 20),
    )(got_a, got_b, *own)
    parity = [list(range(0, 16, 2)), list(range(1, 16, 2))]
    swapped = lax.all_to_all(coded_terms, "fsdp", 0, 0, axis_index_groups=parity, tiled=True)
    sums = pl.pallas_call(
        block_kernel,
        out_shape=jax.ShapeDtypeStruct((8, 64, 128), f32),
        in_specs=[SMEM, VMEM],
        out_specs=VMEM,
        compiler_params=pltpu.CompilerParams(vmem_limit_bytes=16 << 20),
    )(ranking, swapped)
    along_z = [list(range(0, 16, 2)), list(range(1, 16, 2))]
    pieces = lax.all_to_all(sums, "cand", 0, 0, axis_index_groups=along_z, tiled=True)
    beside = lax.ppermute(pieces, "cand", sibling)
    share, loss = pl.pallas_call(
        slope_kernel,
        out_shape=(jax.ShapeDtypeStruct((56, 128), f32), jax.ShapeDtypeStruct((8, 128), f32)),
        in_specs=[VMEM, VMEM],
        out_specs=(VMEM, VMEM),
        compiler_params=pltpu.CompilerParams(vmem_limit_bytes=16 << 20),
    )(pieces, beside)
    share = share + lax.ppermute(share, "prompt", [(0, 1), (1, 0)])
    final = jnp.broadcast_to(share[None], (8, 56, 128))
    final = lax.all_to_all(final, "cand", 0, 0, axis_index_groups=along_z, tiled=True).reshape(448, 128)
    half = BW + BW // 2
    slab_a, slab_b = final[:BW], final[BW:half]
    pooled = final[half : half + 3].reshape(-1)[:BW]
    down_grad = slab_a[:, :R].T
    up_low = jnp.concatenate([slab_b[:, :64], slab_b[:, 64:]], axis=0)
    up_grad = jnp.concatenate([up_low, slab_a[:, R:]], axis=1).T
    gain_f, head_f = gain.astype(f32), head.astype(f32)
    return (loss[0, :1], down_grad, up_grad, head_f * pooled, gain_f * pooled)


def solution(mesh):
    placed = (
        P("prompt", "cand", "fsdp", None),
        P("prompt", "cand"),
        P("prompt", "cand"),
        P("prompt", None),
        P(None, "fsdp"),
        P(None, "fsdp"),
        P("fsdp"),
        P("fsdp"),
    )
    return jax.shard_map(
        on_device,
        mesh=mesh,
        in_specs=placed,
        out_specs=(P("prompt"), P(None, "fsdp"), P(None, "fsdp"), P("fsdp"), P("fsdp")),
        check_vma=False,
    )
```

```python
import jax
import jax.numpy as jnp
from jax import lax
from jax.experimental import pallas as pl
from jax.experimental.pallas import tpu as pltpu
from jax.sharding import PartitionSpec as P

loss_scale = 256.0
D = 4608
R = 96
TOK = 512
NB = 16
BW = 288
HALF = 2304
CH = 512
CUT = 224
STEPS = 32760.0
FINE = 60000.0
TINY = 1e-36
f32 = jnp.float32
bf16 = jnp.bfloat16
VMEM = pl.BlockSpec(memory_space=pltpu.VMEM)
SMEM = pl.BlockSpec(memory_space=pltpu.SMEM)


def mm(a, b, ca, cb):
    return lax.dot_general(a, b, (((ca,), (cb,)), ((), ())), preferred_element_type=f32)


def halves(v):
    hi = v.astype(bf16)
    return hi, (v - hi.astype(f32)).astype(bf16)


def lanes(shape):
    return lax.broadcasted_iota(jnp.int32, shape, len(shape) - 1)


def level(most):
    return jnp.ceil(jnp.log2(jnp.maximum(most, TINY)) * 8.0)


def coded(v, e):
    return jnp.round(v * jnp.exp2(e * -0.125) * STEPS).astype(jnp.int32)


def told_row(part):
    e = level(jnp.abs(part))
    v = part * jnp.exp2(e * -0.125) * STEPS
    hi = jnp.round(v)
    lo = jnp.round((v - hi) * FINE)
    one = lanes((1, 128))
    return jnp.where(one == 0, e, jnp.where(one == 1, hi, jnp.where(one == 2, lo, 0.0))).astype(jnp.int32)


def told(m, scale):
    one = lanes((1, 128))
    v = jnp.where(one == 1, m[6:7], jnp.where(one == 2, m[6:7] * (1.0 / FINE), 0.0))
    by = jnp.sum(jnp.where(one == 0, scale[6:7], 0.0), axis=1, keepdims=True)
    return jnp.sum(v, axis=1, keepdims=True) * (by * (1.0 / STEPS))


def meta_rows(a_e, b_e, window, s_row):
    p_e = level(jnp.max(jnp.abs(window), axis=1, keepdims=True))
    p_q = coded(window, p_e)
    rows = (
        a_e.astype(jnp.int32),
        b_e.astype(jnp.int32),
        p_q[0:1, :128],
        p_q[0:1, 128:256],
        p_q[0:1, 256:384],
        jnp.broadcast_to(p_e[0:1].astype(jnp.int32), (1, 128)),
        s_row,
    )
    at = lax.broadcasted_iota(jnp.int32, (16, 128), 0)
    meta = jnp.zeros((16, 128), jnp.int32)
    for k, r in enumerate(rows):
        meta = jnp.where(at == k, r, meta)
    return meta.astype(jnp.int16)


def pack_kernel(w_ref, out_ref):
    w = w_ref[...].astype(f32)
    w = jnp.concatenate([w, jnp.zeros((128, 96), f32)], axis=1)
    t = jnp.transpose(w)
    lane = lanes((64, 128))
    last = t[224:288]
    for i in range(3):
        cut = slice(64 * i, 64 * i + 64)
        rows = jnp.where(lane < R, t[cut], pltpu.roll(last, 96 - 32 * i, 1)).astype(bf16)
        for j in range(8):
            out_ref[j, cut, :] = rows
    lane = lanes((32, 128))
    rows = jnp.where(lane < R, t[192:224], 0.0)
    for k in range(9):
        piece = t[32 * k : 32 * k + 32]
        rows = jnp.where(lane == R + k, pltpu.roll(piece, k, 1) if k else piece, rows)
    rows = rows.astype(bf16)
    for j in range(8):
        out_ref[j, 192:, :] = rows


def unpack(q_ref, store):
    for j in range(8):
        q = q_ref[j].astype(f32)
        lane = lanes((32, 128))
        part = q[192:]
        cols = [pltpu.roll(part, 128 - k, 1) if k else part for k in range(9)]
        for k in range(7):
            rows = jnp.where(lane < R, q[32 * k : 32 * k + 32], jnp.where(lane == R, cols[k], 0.0))
            store(j * BW + 32 * k, rows.astype(bf16))
        for k in range(2):
            cut = [pltpu.roll(q[64 * i + 32 * k : 64 * i + 32 * k + 32], 32 * i + 32, 1) for i in range(3)]
            rows = jnp.where(lane < 32, cut[0], jnp.where(lane < 64, cut[1], cut[2]))
            rows = jnp.where(lane < R, rows, jnp.where(lane == R, cols[7 + k], 0.0))
            store(j * BW + 224 + 32 * k, rows.astype(bf16))


def unpack_both(core, mine_ref, other_ref, w_ref):
    def stores(left):
        def to_left(at, rows):
            w_ref[at : at + 32, :128] = rows

        def to_right(at, rows):
            w_ref[at : at + 32, 128:] = rows

        return (to_left, to_right) if left else (to_right, to_left)

    for left in (True, False):

        @pl.when((core == 0) == left)
        def _(left=left):
            first, second = stores(left)
            unpack(mine_ref, first)
            unpack(other_ref, second)


def near_kernel(x_ref, mine_ref, other_ref, w_ref, prod_ref, gram_ref, ss_ref):
    unpack_both(lax.axis_index("cand") % 2, mine_ref, other_ref, w_ref)

    def square(i, carry):
        at = pl.ds(pl.multiple_of(i * 16, 16), 16)
        rows = x_ref[at, :].astype(f32)
        ss_ref[at, :] = jnp.broadcast_to(jnp.sum(rows * rows, axis=1, keepdims=True), (16, 128))
        return carry

    lax.fori_loop(0, TOK // 16, square, 0)
    cols = pl.ds(pl.multiple_of(lax.axis_index("fsdp") // 8 * HALF, 128), HALF)
    prod_ref[...] = mm(x_ref[:, cols], w_ref[...], 1, 0)
    gram_ref[...] = mm(w_ref[...], w_ref[...], 0, 0)


def local_kernel(
    starts,
    lengths,
    x_ref,
    w_near,
    prod_near,
    gram_near,
    ss_ref,
    mine_ref,
    other_ref,
    send_a,
    send_b,
    own_a,
    own_b,
    own_p,
    own_s,
    w_far,
    w_ref,
    g_ref,
    p_ref,
):
    start, length = starts[0, 0], lengths[0, 0]
    first = lax.axis_index("fsdp") * TOK
    core = lax.axis_index("cand") % 2
    side = lax.axis_index("fsdp") // 8
    unpack_both(core, mine_ref, other_ref, w_far)
    w_ref[pl.ds(pl.multiple_of(side * HALF, 256), HALF), :] = w_near[...]
    w_ref[pl.ds(pl.multiple_of((1 - side) * HALF, 256), HALF), :] = w_far[...]
    cols = pl.ds(pl.multiple_of((1 - side) * HALF, 128), HALF)
    prod = prod_near[...] + mm(x_ref[:, cols], w_far[...], 1, 0)
    gram = gram_near[...] + mm(w_far[...], w_far[...], 0, 0)
    pre = prod[:, :128]
    x_up = prod[:, 128:]
    lane = lanes((TOK, 128))
    unit = lane < R
    sig = 1.0 / (1.0 + jnp.exp(-pre))
    act_b = jnp.where(unit, pre * sig, 0.0).astype(bf16)
    act = act_b.astype(f32)
    g_hi, g_lo = halves(gram[128:, :])
    through = mm(act_b, g_hi, 1, 0) + mm(act_b, g_lo, 1, 0)
    m_left = pre + through[:, :128]
    m_up = x_up + through[:, 128:]
    m_head = jnp.sum(jnp.where(lane == R, m_left + m_up, 0.0), axis=1, keepdims=True)
    m_sq = ss_ref[:, :1] + jnp.sum(act * (x_up + m_up), axis=1, keepdims=True)
    inv = lax.rsqrt(jnp.maximum(m_sq, 0.0) * (1.0 / D) + 1e-06)
    score = inv * m_head
    count = (length - start).astype(f32)
    pos = first + lax.broadcasted_iota(jnp.int32, (TOK, 1), 0)
    valid = (pos >= start) & (pos < length)
    part = jnp.sum(jnp.where(valid, score, 0.0), axis=0, keepdims=True) / count
    weight = jnp.where(valid, loss_scale / count, 0.0)
    alpha = inv * weight
    beta = inv * inv * weight * score * (1.0 / D)
    up_head = gram[R : R + 1, 128:] + gram[128 + R : 129 + R, 128:]
    back = alpha * up_head - beta * m_up
    pre_grad = back * sig * (1.0 + pre * (1.0 - sig))
    nab = -(act * beta)
    left = jnp.where(unit, pre_grad, pltpu.roll(nab, 32, 1))
    right = jnp.where(lane < 64, nab, pltpu.roll(nab, 64, 1))
    lhs = jnp.concatenate([left, right], axis=1).astype(bf16)
    a_left = jnp.where(unit, 0.0, pltpu.roll(act, 32, 1))
    a_right = jnp.where(lane < 64, act, pltpu.roll(act, 64, 1))
    u_row = jnp.sum(alpha * jnp.concatenate([a_left, a_right], axis=1), axis=0, keepdims=True)
    v_row = jnp.sum(alpha * act, axis=0, keepdims=True)
    low = mm(act_b, lhs, 0, 0)
    low = jnp.where(lanes((128, 256)) < R, 0.0, low)
    row = lax.broadcasted_iota(jnp.int32, (128, 256), 0)
    top = jnp.where(row == R, u_row, 0.0)
    low = jnp.where(row == R, u_row, low)
    c_hi, c_lo = halves(jnp.concatenate([top, low], axis=0))
    for i in range(D // CH):
        cut = slice(i * CH, (i + 1) * CH)
        w = w_ref[cut, :]
        g_ref[cut, :] = mm(x_ref[:, cut], lhs, 0, 0) + (mm(w, c_hi, 1, 0) + mm(w, c_lo, 1, 0))

    al_hi = alpha.astype(bf16).astype(f32)
    al_lo = alpha - al_hi
    al = jnp.where(lane == 0, al_hi, jnp.where(lane == 1, al_lo, 0.0))
    al = jnp.transpose(al)[:16].astype(bf16)
    v_hi = v_row.astype(bf16).astype(f32)
    row = lax.broadcasted_iota(jnp.int32, (16, 128), 0)
    vv = jnp.where(row == 0, v_hi, jnp.where(row == 1, v_row - v_hi, 0.0)).astype(bf16)
    pooled = mm(al, x_ref[...], 1, 0) + mm(vv, w_ref[:, 128:], 1, 1)
    p_ref[:, D:] = jnp.zeros((8, 256), f32)
    p_ref[:, :D] = jnp.broadcast_to(pooled[0:1] + pooled[1:2], (8, D))

    def window(j):
        base = j * BW // 128 * 128
        off = j * BW - base
        w = p_ref[:, base : base + 512]
        if off:
            w = pltpu.roll(w, 512 - off, 1)
        return jnp.where(lanes((8, 512)) < BW, w, 0.0)

    def block(j):
        a = g_ref[pl.ds(pl.multiple_of(j * BW, 32), BW), :128]
        b0 = g_ref[pl.ds(pl.multiple_of(j * BW, 32), BW // 2), 128:]
        b1 = g_ref[pl.ds(pl.multiple_of(j * BW + BW // 2, 16), BW // 2), 128:]
        return a, jnp.where(lanes((BW // 2, 128)) < 64, b0, b1)

    par = lax.axis_index("fsdp") % 2
    s_row = told_row(part)
    own_s[...] = jnp.broadcast_to(part, (8, 128))
    for i in range(8):
        even, odd = window(2 * i), window(2 * i + 1)
        a, b = block(2 * i + 1 - par)
        a_e = level(jnp.max(jnp.abs(a), axis=0, keepdims=True))
        b_e = level(jnp.max(jnp.abs(b), axis=0, keepdims=True))
        q = coded(a, a_e).astype(jnp.int16)
        meta = meta_rows(a_e, b_e, jnp.where(par == 0, odd, even), s_row)
        send_a[i, :CUT, :] = q[:CUT]
        send_a[i, CUT:, :] = meta
        send_b[i, : BW - CUT, :] = q[CUT:]
        send_b[i, BW - CUT : BW - CUT + BW // 2, :] = coded(b, b_e).astype(jnp.int16)
        send_b[i, BW - CUT + BW // 2 :, :] = meta
        a, b = block(2 * i + par)
        own_a[i] = a
        own_b[i] = b
        own_p[i] = jnp.where(par == 0, even, odd)


def pair_kernel(got_a, got_b, own_a, own_b, own_p, own_s, out_ref):
    end = BW - CUT + BW // 2
    m_a = [got_a[i, CUT:, :].astype(jnp.int32).astype(f32) for i in range(8)]
    m_b = [got_b[i, end:, :].astype(jnp.int32).astype(f32) for i in range(8)]
    scale = jnp.exp2(m_b[0] * 0.125)
    s_row = told_row(own_s[0:1, 0:1] + told(m_b[0], scale))
    for i in range(8):
        by_a = jnp.exp2(m_a[i][0:1] * 0.125) * (1.0 / STEPS)
        by = jnp.exp2(m_b[i] * 0.125) * (1.0 / STEPS)
        top = own_a[i, :CUT] + got_a[i, :CUT, :].astype(jnp.int32).astype(f32) * by_a
        low = own_a[i, CUT:] + got_b[i, : BW - CUT, :].astype(jnp.int32).astype(f32) * by[0:1]
        b = own_b[i] + got_b[i, BW - CUT : end, :].astype(jnp.int32).astype(f32) * by[1:2]
        m = m_b[i]
        got_p = jnp.concatenate([m[2:3], m[3:4], m[4:5], jnp.zeros((1, 128), f32)], axis=1)
        p = own_p[i] + got_p * jnp.concatenate([by[5:6]] * 4, axis=1)
        most = jnp.maximum(
            jnp.max(jnp.abs(top), axis=0, keepdims=True), jnp.max(jnp.abs(low), axis=0, keepdims=True)
        )
        a_e = level(most)
        b_e = level(jnp.max(jnp.abs(b), axis=0, keepdims=True))
        out_ref[i, :CUT, :] = coded(top, a_e).astype(jnp.int16)
        out_ref[i, CUT:BW, :] = coded(low, a_e).astype(jnp.int16)
        out_ref[i, BW : BW + BW // 2, :] = coded(b, b_e).astype(jnp.int16)
        out_ref[i, BW + BW // 2 :, :] = meta_rows(a_e, b_e, p, s_row)


def block_kernel(ranking, q_ref, out_ref):
    mine = lax.axis_index("cand")
    place = jnp.int32(0)
    for k in range(16):
        place = jnp.where(ranking[0, k] == mine, jnp.int32(k), place)
    half = BW + BW // 2
    parts = [q_ref[s, half:, :].astype(jnp.int32).astype(f32) for s in range(8)]
    scale = [jnp.exp2(m * 0.125) for m in parts]
    pooled = [jnp.zeros((1, 128), f32) for _ in range(3)]
    reward = jnp.zeros((1, 1), f32)
    one = lanes((1, 128))
    for s in range(8):
        m, e = parts[s], scale[s] * (1.0 / STEPS)
        for k in range(3):
            pooled[k] = pooled[k] + m[2 + k : 3 + k] * e[5:6]
        reward = reward + told(m, scale[s])
    at = lax.broadcasted_iota(jnp.int32, (16, 128), 0)
    tail = jnp.zeros((16, 128), f32)
    for k in range(3):
        tail = jnp.where(at == k, pooled[k], tail)
    meta = jnp.where(one < 64, reward, place.astype(f32))
    meta = jnp.broadcast_to(meta, (8, 128))
    for i in range(28):
        if i < half // 16:
            which = 0 if i < BW // 16 else 1
            acc = jnp.zeros((16, 128), f32)
            for s in range(8):
                v = q_ref[s, i * 16 : (i + 1) * 16, :].astype(jnp.int32).astype(f32)
                acc = acc + v * (scale[s][which : which + 1] * (1.0 / STEPS))
        else:
            acc = tail
        for g in (2 * i, 2 * i + 1):
            at = g % 7 * 8
            out_ref[g // 7, at : at + 8, :] = acc[g % 2 * 8 : g % 2 * 8 + 8]
    for i in range(8):
        out_ref[i, 56:, :] = meta


def slope_kernel(d_ref, o_ref, out_ref, loss_ref):
    told = jnp.concatenate([d_ref[:, 56, :], o_ref[:, 56, :]], axis=0)
    lane = lanes((16, 128))
    row = lax.broadcasted_iota(jnp.int32, (16, 128), 0)
    r_col = jnp.sum(jnp.where(lane == 0, told, 0.0), axis=1, keepdims=True)
    k_col = jnp.sum(jnp.where(lane == 64, told, 0.0), axis=1, keepdims=True)
    r_row = jnp.sum(jnp.where(lane == row, r_col, 0.0), axis=0, keepdims=True)
    k_row = jnp.sum(jnp.where(lane == row, k_col, 0.0), axis=0, keepdims=True)
    real = lane < 16
    later = real & (k_col >= k_row)
    top = jnp.max(jnp.where(later, r_col, -1e30), axis=0, keepdims=True)
    top = jnp.where(real[0:1], top, 0.0)
    ex = jnp.where(later, jnp.exp(jnp.where(later, r_col - top, 0.0)), 0.0)
    total = jnp.where(real[0:1], jnp.sum(ex, axis=0, keepdims=True), 1.0)
    slope = jnp.sum(ex / total, axis=1, keepdims=True) - 1.0
    terms = jnp.where(real[0:1], top + jnp.log(total) - r_row, 0.0)
    loss_ref[...] = jnp.broadcast_to(jnp.sum(terms, axis=1, keepdims=True), (8, 128))
    acc = jnp.zeros((56, 128), f32)
    for i in range(8):
        acc = acc + d_ref[i, :56, :] * slope[i : i + 1] + o_ref[i, :56, :] * slope[8 + i : 9 + i]
    out_ref[...] = acc


def both_kernel(a_ref, b_ref, out_ref):
    both = a_ref[...] + b_ref[...]
    for i in range(8):
        out_ref[i] = both


def out_kernel(in_ref, down_ref, up_ref):
    pad = jnp.zeros((384 - BW, 128), f32)
    first = jnp.transpose(jnp.concatenate([in_ref[:BW], pad], axis=0))
    low = in_ref[BW : BW + BW // 2]
    low = jnp.transpose(jnp.concatenate([low, pltpu.roll(low, 64, 1), pad], axis=0))
    down_ref[...] = first[:R, :BW]
    up_ref[:64, :] = low[:64, :BW]
    up_ref[64:, :] = first[R:, :BW]


def on_device(hidden, lengths, starts, ranking, down_w, up_w, gain, head):
    x = hidden[0, 0]
    core = lax.axis_index("cand") % 2
    sibling = [(i, i ^ 1) for i in range(16)]
    both = gain.astype(f32) * head.astype(f32)
    near = lax.reduce_precision(both, 8, 7)
    part = jnp.where(core == 0, near, both - near).astype(bf16)
    half_w = jnp.where(core == 0, down_w, up_w)
    half_w = jnp.concatenate([half_w, jnp.broadcast_to(part[None], (32, BW))], axis=0)
    packed = pl.pallas_call(
        pack_kernel,
        out_shape=jax.ShapeDtypeStruct((8, 224, 128), bf16),
        in_specs=[VMEM],
        out_specs=VMEM,
        compiler_params=pltpu.CompilerParams(vmem_limit_bytes=16 << 20),
    )(half_w)
    along_y = [list(range(8)), list(range(8, 16))]
    mine = lax.all_to_all(packed, "fsdp", 0, 0, axis_index_groups=along_y, tiled=True)
    across = [(i, i ^ 8) for i in range(16)]
    far_mine = lax.ppermute(mine, "fsdp", across)
    other = lax.ppermute(mine, "cand", sibling)
    w_near, prod, gram, squares = pl.pallas_call(
        near_kernel,
        out_shape=(
            jax.ShapeDtypeStruct((HALF, 256), bf16),
            jax.ShapeDtypeStruct((TOK, 256), f32),
            jax.ShapeDtypeStruct((256, 256), f32),
            jax.ShapeDtypeStruct((TOK, 128), f32),
        ),
        in_specs=[VMEM, VMEM, VMEM],
        out_specs=(VMEM, VMEM, VMEM, VMEM),
        compiler_params=pltpu.CompilerParams(vmem_limit_bytes=24 << 20),
    )(x, mine, other)
    far_mine, squares = lax.optimization_barrier((far_mine, squares))
    far_other = lax.ppermute(far_mine, "cand", sibling)
    rows = BW + BW // 2 + 16
    send_a, send_b, *own = pl.pallas_call(
        local_kernel,
        out_shape=(
            jax.ShapeDtypeStruct((8, CUT + 16, 128), jnp.int16),
            jax.ShapeDtypeStruct((8, rows - CUT, 128), jnp.int16),
            jax.ShapeDtypeStruct((8, BW, 128), f32),
            jax.ShapeDtypeStruct((8, BW // 2, 128), f32),
            jax.ShapeDtypeStruct((8, 8, 512), f32),
            jax.ShapeDtypeStruct((8, 128), f32),
        ),
        in_specs=[SMEM, SMEM] + [VMEM] * 7,
        out_specs=(VMEM,) * 6,
        scratch_shapes=[
            pltpu.VMEM((HALF, 256), bf16),
            pltpu.VMEM((D, 256), bf16),
            pltpu.VMEM((D, 256), f32),
            pltpu.VMEM((8, D + 256), f32),
        ],
        compiler_params=pltpu.CompilerParams(vmem_limit_bytes=40 << 20),
    )(starts, lengths, x, w_near, prod, gram, squares, far_mine, far_other)
    got_a = lax.ppermute(send_a, "fsdp", [(i, i ^ 1) for i in range(16)])
    turn = [(i, i // 8 * 8 + (i + (1 if i % 2 else 7)) % 8) for i in range(16)]
    got_b = lax.ppermute(send_b, "fsdp", turn)
    coded_terms = pl.pallas_call(
        pair_kernel,
        out_shape=jax.ShapeDtypeStruct((8, rows, 128), jnp.int16),
        in_specs=[VMEM] * 6,
        out_specs=VMEM,
        compiler_params=pltpu.CompilerParams(vmem_limit_bytes=24 << 20),
    )(got_a, got_b, *own)
    parity = [list(range(0, 16, 2)), list(range(1, 16, 2))]
    swapped = lax.all_to_all(coded_terms, "fsdp", 0, 0, axis_index_groups=parity, tiled=True)
    sums = pl.pallas_call(
        block_kernel,
        out_shape=jax.ShapeDtypeStruct((8, 64, 128), f32),
        in_specs=[SMEM, VMEM],
        out_specs=VMEM,
        compiler_params=pltpu.CompilerParams(vmem_limit_bytes=16 << 20),
    )(ranking, swapped)
    along_z = [list(range(0, 16, 2)), list(range(1, 16, 2))]
    pieces = lax.all_to_all(sums, "cand", 0, 0, axis_index_groups=along_z, tiled=True)
    beside = lax.ppermute(pieces, "cand", sibling)
    share, loss = pl.pallas_call(
        slope_kernel,
        out_shape=(jax.ShapeDtypeStruct((56, 128), f32), jax.ShapeDtypeStruct((8, 128), f32)),
        in_specs=[VMEM, VMEM],
        out_specs=(VMEM, VMEM),
        compiler_params=pltpu.CompilerParams(vmem_limit_bytes=16 << 20),
    )(pieces, beside)
    final = pl.pallas_call(
        both_kernel,
        out_shape=jax.ShapeDtypeStruct((8, 56, 128), f32),
        in_specs=[VMEM, VMEM],
        out_specs=VMEM,
        compiler_params=pltpu.CompilerParams(vmem_limit_bytes=16 << 20),
    )(share, lax.ppermute(share, "prompt", [(0, 1), (1, 0)]))
    final = lax.all_to_all(final, "cand", 0, 0, axis_index_groups=along_z, tiled=True).reshape(448, 128)
    down_grad, up_grad = pl.pallas_call(
        out_kernel,
        out_shape=(jax.ShapeDtypeStruct((R, BW), f32), jax.ShapeDtypeStruct((R, BW), f32)),
        in_specs=[VMEM],
        out_specs=(VMEM, VMEM),
        compiler_params=pltpu.CompilerParams(vmem_limit_bytes=16 << 20),
    )(final)
    half = BW + BW // 2
    pooled = final[half : half + 3].reshape(-1)[:BW]
    gain_f, head_f = gain.astype(f32), head.astype(f32)
    return (loss[0, :1], down_grad, up_grad, head_f * pooled, gain_f * pooled)


def solution(mesh):
    placed = (
        P("prompt", "cand", "fsdp", None),
        P("prompt", "cand"),
        P("prompt", "cand"),
        P("prompt", None),
        P(None, "fsdp"),
        P(None, "fsdp"),
        P("fsdp"),
        P("fsdp"),
    )
    return jax.shard_map(
        on_device,
        mesh=mesh,
        in_specs=placed,
        out_specs=(P("prompt"), P(None, "fsdp"), P(None, "fsdp"), P("fsdp"), P("fsdp")),
        check_vma=False,
    )
```

```python
import jax
import jax.numpy as jnp
from jax import lax
from jax.experimental import pallas as pl
from jax.experimental.pallas import tpu as pltpu
from jax.sharding import PartitionSpec as P

loss_scale = 256.0
D = 4608
R = 96
TOK = 512
NB = 16
BW = 288
HALF = 2304
CH = 512
CUT = 224
STEPS = 32760.0
FINE = 60000.0
TINY = 1e-36
f32 = jnp.float32
bf16 = jnp.bfloat16
VMEM = pl.BlockSpec(memory_space=pltpu.VMEM)
SMEM = pl.BlockSpec(memory_space=pltpu.SMEM)


def mm(a, b, ca, cb):
    return lax.dot_general(a, b, (((ca,), (cb,)), ((), ())), preferred_element_type=f32)


def halves(v):
    hi = v.astype(bf16)
    return hi, (v - hi.astype(f32)).astype(bf16)


def lanes(shape):
    return lax.broadcasted_iota(jnp.int32, shape, len(shape) - 1)


def level(most):
    return jnp.ceil(jnp.log2(jnp.maximum(most, TINY)) * 8.0)


def coded(v, e):
    return jnp.round(v * jnp.exp2(e * -0.125) * STEPS).astype(jnp.int32)


def told_row(part):
    e = level(jnp.abs(part))
    v = part * jnp.exp2(e * -0.125) * STEPS
    hi = jnp.round(v)
    lo = jnp.round((v - hi) * FINE)
    one = lanes((1, 128))
    return jnp.where(one == 0, e, jnp.where(one == 1, hi, jnp.where(one == 2, lo, 0.0))).astype(jnp.int32)


def told(m, scale):
    one = lanes((1, 128))
    v = jnp.where(one == 1, m[6:7], jnp.where(one == 2, m[6:7] * (1.0 / FINE), 0.0))
    by = jnp.sum(jnp.where(one == 0, scale[6:7], 0.0), axis=1, keepdims=True)
    return jnp.sum(v, axis=1, keepdims=True) * (by * (1.0 / STEPS))


def meta_rows(a_e, b_e, window, s_row):
    p_e = level(jnp.max(jnp.abs(window), axis=1, keepdims=True))
    p_q = coded(window, p_e)
    rows = (
        a_e.astype(jnp.int32),
        b_e.astype(jnp.int32),
        p_q[0:1, :128],
        p_q[0:1, 128:256],
        p_q[0:1, 256:384],
        jnp.broadcast_to(p_e[0:1].astype(jnp.int32), (1, 128)),
        s_row,
    )
    at = lax.broadcasted_iota(jnp.int32, (16, 128), 0)
    meta = jnp.zeros((16, 128), jnp.int32)
    for k, r in enumerate(rows):
        meta = jnp.where(at == k, r, meta)
    return meta.astype(jnp.int16)


def pack_kernel(w_ref, out_ref):
    w = w_ref[...].astype(f32)
    w = jnp.concatenate([w, jnp.zeros((128, 96), f32)], axis=1)
    t = jnp.transpose(w)
    lane = lanes((64, 128))
    last = t[224:288]
    for i in range(3):
        cut = slice(64 * i, 64 * i + 64)
        rows = jnp.where(lane < R, t[cut], pltpu.roll(last, 96 - 32 * i, 1)).astype(bf16)
        for j in range(8):
            out_ref[j, cut, :] = rows
    lane = lanes((32, 128))
    rows = jnp.where(lane < R, t[192:224], 0.0)
    for k in range(9):
        piece = t[32 * k : 32 * k + 32]
        rows = jnp.where(lane == R + k, pltpu.roll(piece, k, 1) if k else piece, rows)
    rows = rows.astype(bf16)
    for j in range(8):
        out_ref[j, 192:, :] = rows


def unpack(q_ref, store):
    for j in range(8):
        q = q_ref[j].astype(f32)
        lane = lanes((32, 128))
        part = q[192:]
        cols = [pltpu.roll(part, 128 - k, 1) if k else part for k in range(9)]
        for k in range(7):
            rows = jnp.where(lane < R, q[32 * k : 32 * k + 32], jnp.where(lane == R, cols[k], 0.0))
            store(j * BW + 32 * k, rows.astype(bf16))
        for k in range(2):
            cut = [pltpu.roll(q[64 * i + 32 * k : 64 * i + 32 * k + 32], 32 * i + 32, 1) for i in range(3)]
            rows = jnp.where(lane < 32, cut[0], jnp.where(lane < 64, cut[1], cut[2]))
            rows = jnp.where(lane < R, rows, jnp.where(lane == R, cols[7 + k], 0.0))
            store(j * BW + 224 + 32 * k, rows.astype(bf16))


def unpack_both(core, mine_ref, other_ref, w_ref):
    def stores(left):
        def to_left(at, rows):
            w_ref[at : at + 32, :128] = rows

        def to_right(at, rows):
            w_ref[at : at + 32, 128:] = rows

        return (to_left, to_right) if left else (to_right, to_left)

    for left in (True, False):

        @pl.when((core == 0) == left)
        def _(left=left):
            first, second = stores(left)
            unpack(mine_ref, first)
            unpack(other_ref, second)


def near_kernel(x_ref, mine_ref, other_ref, w_ref, prod_ref, gram_ref, ss_ref, t_ref):
    unpack_both(lax.axis_index("cand") % 2, mine_ref, other_ref, w_ref)

    def square(i, carry):
        at = pl.ds(pl.multiple_of(i * 16, 16), 16)
        rows = x_ref[at, :].astype(f32)
        ss_ref[at, :] = jnp.broadcast_to(jnp.sum(rows * rows, axis=1, keepdims=True), (16, 128))
        return carry

    lax.fori_loop(0, TOK // 16, square, 0)
    cols = pl.ds(pl.multiple_of(lax.axis_index("fsdp") // 8 * HALF, 128), HALF)
    prod_ref[...] = mm(x_ref[:, cols], w_ref[...], 1, 0)
    for i in range(D // CH):
        cut = slice(i * CH, (i + 1) * CH)
        t_ref[cut, :] = jnp.transpose(x_ref[:, cut])
    gram_ref[...] = mm(w_ref[...], w_ref[...], 0, 0)


def local_kernel(
    starts,
    lengths,
    x_ref,
    w_near,
    prod_near,
    gram_near,
    ss_ref,
    t_ref,
    mine_ref,
    other_ref,
    send_a,
    send_b,
    own_a,
    own_b,
    own_p,
    own_s,
    w_far,
    w_ref,
    g_ref,
    p_ref,
):
    start, length = starts[0, 0], lengths[0, 0]
    first = lax.axis_index("fsdp") * TOK
    core = lax.axis_index("cand") % 2
    side = lax.axis_index("fsdp") // 8
    unpack_both(core, mine_ref, other_ref, w_far)
    w_ref[pl.ds(pl.multiple_of(side * HALF, 256), HALF), :] = w_near[...]
    w_ref[pl.ds(pl.multiple_of((1 - side) * HALF, 256), HALF), :] = w_far[...]
    cols = pl.ds(pl.multiple_of((1 - side) * HALF, 128), HALF)
    prod = prod_near[...] + mm(x_ref[:, cols], w_far[...], 1, 0)
    gram = gram_near[...] + mm(w_far[...], w_far[...], 0, 0)
    pre = prod[:, :128]
    x_up = prod[:, 128:]
    lane = lanes((TOK, 128))
    unit = lane < R
    sig = 1.0 / (1.0 + jnp.exp(-pre))
    act_b = jnp.where(unit, pre * sig, 0.0).astype(bf16)
    act = act_b.astype(f32)
    g_hi, g_lo = halves(gram[128:, :])
    through = mm(act_b, g_hi, 1, 0) + mm(act_b, g_lo, 1, 0)
    m_left = pre + through[:, :128]
    m_up = x_up + through[:, 128:]
    m_head = jnp.sum(jnp.where(lane == R, m_left + m_up, 0.0), axis=1, keepdims=True)
    m_sq = ss_ref[:, :1] + jnp.sum(act * (x_up + m_up), axis=1, keepdims=True)
    inv = lax.rsqrt(jnp.maximum(m_sq, 0.0) * (1.0 / D) + 1e-06)
    score = inv * m_head
    count = (length - start).astype(f32)
    pos = first + lax.broadcasted_iota(jnp.int32, (TOK, 1), 0)
    valid = (pos >= start) & (pos < length)
    part = jnp.sum(jnp.where(valid, score, 0.0), axis=0, keepdims=True) / count
    weight = jnp.where(valid, loss_scale / count, 0.0)
    alpha = inv * weight
    beta = inv * inv * weight * score * (1.0 / D)
    up_head = gram[R : R + 1, 128:] + gram[128 + R : 129 + R, 128:]
    back = alpha * up_head - beta * m_up
    pre_grad = back * sig * (1.0 + pre * (1.0 - sig))
    nab = -(act * beta)
    left = jnp.where(unit, pre_grad, pltpu.roll(nab, 32, 1))
    right = jnp.where(lane < 64, nab, pltpu.roll(nab, 64, 1))
    lhs = jnp.concatenate([left, right], axis=1).astype(bf16)
    a_left = jnp.where(unit, 0.0, pltpu.roll(act, 32, 1))
    a_right = jnp.where(lane < 64, act, pltpu.roll(act, 64, 1))
    u_row = jnp.sum(alpha * jnp.concatenate([a_left, a_right], axis=1), axis=0, keepdims=True)
    v_row = jnp.sum(alpha * act, axis=0, keepdims=True)
    low = mm(act_b, lhs, 0, 0)
    low = jnp.where(lanes((128, 256)) < R, 0.0, low)
    row = lax.broadcasted_iota(jnp.int32, (128, 256), 0)
    top = jnp.where(row == R, u_row, 0.0)
    low = jnp.where(row == R, u_row, low)
    c_hi, c_lo = halves(jnp.concatenate([top, low], axis=0))
    for i in range(D // CH):
        cut = slice(i * CH, (i + 1) * CH)
        w = w_ref[cut, :]
        g_ref[cut, :] = mm(t_ref[cut, :], lhs, 1, 0) + (mm(w, c_hi, 1, 0) + mm(w, c_lo, 1, 0))

    al_hi = alpha.astype(bf16).astype(f32)
    al_lo = alpha - al_hi
    al = jnp.where(lane == 0, al_hi, jnp.where(lane == 1, al_lo, 0.0))
    al = jnp.transpose(al)[:16].astype(bf16)
    v_hi = v_row.astype(bf16).astype(f32)
    row = lax.broadcasted_iota(jnp.int32, (16, 128), 0)
    vv = jnp.where(row == 0, v_hi, jnp.where(row == 1, v_row - v_hi, 0.0)).astype(bf16)
    pooled = mm(al, x_ref[...], 1, 0) + mm(vv, w_ref[:, 128:], 1, 1)
    p_ref[:, D:] = jnp.zeros((8, 256), f32)
    p_ref[:, :D] = jnp.broadcast_to(pooled[0:1] + pooled[1:2], (8, D))

    def window(j):
        base = j * BW // 128 * 128
        off = j * BW - base
        w = p_ref[:, base : base + 512]
        if off:
            w = pltpu.roll(w, 512 - off, 1)
        return jnp.where(lanes((8, 512)) < BW, w, 0.0)

    def block(j):
        a = g_ref[pl.ds(pl.multiple_of(j * BW, 32), BW), :128]
        b0 = g_ref[pl.ds(pl.multiple_of(j * BW, 32), BW // 2), 128:]
        b1 = g_ref[pl.ds(pl.multiple_of(j * BW + BW // 2, 16), BW // 2), 128:]
        return a, jnp.where(lanes((BW // 2, 128)) < 64, b0, b1)

    par = lax.axis_index("fsdp") % 2
    s_row = told_row(part)
    own_s[...] = jnp.broadcast_to(part, (8, 128))
    for i in range(8):
        even, odd = window(2 * i), window(2 * i + 1)
        a, b = block(2 * i + 1 - par)
        a_e = level(jnp.max(jnp.abs(a), axis=0, keepdims=True))
        b_e = level(jnp.max(jnp.abs(b), axis=0, keepdims=True))
        q = coded(a, a_e).astype(jnp.int16)
        meta = meta_rows(a_e, b_e, jnp.where(par == 0, odd, even), s_row)
        send_a[i, :CUT, :] = q[:CUT]
        send_a[i, CUT:, :] = meta
        send_b[i, : BW - CUT, :] = q[CUT:]
        send_b[i, BW - CUT : BW - CUT + BW // 2, :] = coded(b, b_e).astype(jnp.int16)
        send_b[i, BW - CUT + BW // 2 :, :] = meta
        a, b = block(2 * i + par)
        own_a[i] = a
        own_b[i] = b
        own_p[i] = jnp.where(par == 0, even, odd)


def pair_kernel(got_a, got_b, own_a, own_b, own_p, own_s, out_ref):
    end = BW - CUT + BW // 2
    m_a = [got_a[i, CUT:, :].astype(jnp.int32).astype(f32) for i in range(8)]
    m_b = [got_b[i, end:, :].astype(jnp.int32).astype(f32) for i in range(8)]
    scale = jnp.exp2(m_b[0] * 0.125)
    s_row = told_row(own_s[0:1, 0:1] + told(m_b[0], scale))
    for i in range(8):
        by_a = jnp.exp2(m_a[i][0:1] * 0.125) * (1.0 / STEPS)
        by = jnp.exp2(m_b[i] * 0.125) * (1.0 / STEPS)
        top = own_a[i, :CUT] + got_a[i, :CUT, :].astype(jnp.int32).astype(f32) * by_a
        low = own_a[i, CUT:] + got_b[i, : BW - CUT, :].astype(jnp.int32).astype(f32) * by[0:1]
        b = own_b[i] + got_b[i, BW - CUT : end, :].astype(jnp.int32).astype(f32) * by[1:2]
        m = m_b[i]
        got_p = jnp.concatenate([m[2:3], m[3:4], m[4:5], jnp.zeros((1, 128), f32)], axis=1)
        p = own_p[i] + got_p * jnp.concatenate([by[5:6]] * 4, axis=1)
        most = jnp.maximum(
            jnp.max(jnp.abs(top), axis=0, keepdims=True), jnp.max(jnp.abs(low), axis=0, keepdims=True)
        )
        a_e = level(most)
        b_e = level(jnp.max(jnp.abs(b), axis=0, keepdims=True))
        out_ref[i, :CUT, :] = coded(top, a_e).astype(jnp.int16)
        out_ref[i, CUT:BW, :] = coded(low, a_e).astype(jnp.int16)
        out_ref[i, BW : BW + BW // 2, :] = coded(b, b_e).astype(jnp.int16)
        out_ref[i, BW + BW // 2 :, :] = meta_rows(a_e, b_e, p, s_row)


def block_kernel(ranking, q_ref, out_ref):
    mine = lax.axis_index("cand")
    place = jnp.int32(0)
    for k in range(16):
        place = jnp.where(ranking[0, k] == mine, jnp.int32(k), place)
    half = BW + BW // 2
    parts = [q_ref[s, half:, :].astype(jnp.int32).astype(f32) for s in range(8)]
    scale = [jnp.exp2(m * 0.125) for m in parts]
    pooled = [jnp.zeros((1, 128), f32) for _ in range(3)]
    reward = jnp.zeros((1, 1), f32)
    one = lanes((1, 128))
    for s in range(8):
        m, e = parts[s], scale[s] * (1.0 / STEPS)
        for k in range(3):
            pooled[k] = pooled[k] + m[2 + k : 3 + k] * e[5:6]
        reward = reward + told(m, scale[s])
    at = lax.broadcasted_iota(jnp.int32, (16, 128), 0)
    tail = jnp.zeros((16, 128), f32)
    for k in range(3):
        tail = jnp.where(at == k, pooled[k], tail)
    meta = jnp.where(one < 64, reward, place.astype(f32))
    meta = jnp.broadcast_to(meta, (8, 128))
    for i in range(28):
        if i < half // 16:
            which = 0 if i < BW // 16 else 1
            acc = jnp.zeros((16, 128), f32)
            for s in range(8):
                v = q_ref[s, i * 16 : (i + 1) * 16, :].astype(jnp.int32).astype(f32)
                acc = acc + v * (scale[s][which : which + 1] * (1.0 / STEPS))
        else:
            acc = tail
        for g in (2 * i, 2 * i + 1):
            at = g % 7 * 8
            out_ref[g // 7, at : at + 8, :] = acc[g % 2 * 8 : g % 2 * 8 + 8]
    for i in range(8):
        out_ref[i, 56:, :] = meta


def slope_kernel(d_ref, o_ref, out_ref, loss_ref):
    told = jnp.concatenate([d_ref[:, 56, :], o_ref[:, 56, :]], axis=0)
    lane = lanes((16, 128))
    row = lax.broadcasted_iota(jnp.int32, (16, 128), 0)
    r_col = jnp.sum(jnp.where(lane == 0, told, 0.0), axis=1, keepdims=True)
    k_col = jnp.sum(jnp.where(lane == 64, told, 0.0), axis=1, keepdims=True)
    r_row = jnp.sum(jnp.where(lane == row, r_col, 0.0), axis=0, keepdims=True)
    k_row = jnp.sum(jnp.where(lane == row, k_col, 0.0), axis=0, keepdims=True)
    real = lane < 16
    later = real & (k_col >= k_row)
    top = jnp.max(jnp.where(later, r_col, -1e30), axis=0, keepdims=True)
    top = jnp.where(real[0:1], top, 0.0)
    ex = jnp.where(later, jnp.exp(jnp.where(later, r_col - top, 0.0)), 0.0)
    total = jnp.where(real[0:1], jnp.sum(ex, axis=0, keepdims=True), 1.0)
    slope = jnp.sum(ex / total, axis=1, keepdims=True) - 1.0
    terms = jnp.where(real[0:1], top + jnp.log(total) - r_row, 0.0)
    loss_ref[...] = jnp.broadcast_to(jnp.sum(terms, axis=1, keepdims=True), (8, 128))
    acc = jnp.zeros((56, 128), f32)
    for i in range(8):
        acc = acc + d_ref[i, :56, :] * slope[i : i + 1] + o_ref[i, :56, :] * slope[8 + i : 9 + i]
    out_ref[...] = acc


def both_kernel(a_ref, b_ref, out_ref):
    both = a_ref[...] + b_ref[...]
    for i in range(8):
        out_ref[i] = both


def out_kernel(in_ref, down_ref, up_ref):
    pad = jnp.zeros((384 - BW, 128), f32)
    first = jnp.transpose(jnp.concatenate([in_ref[:BW], pad], axis=0))
    low = in_ref[BW : BW + BW // 2]
    low = jnp.transpose(jnp.concatenate([low, pltpu.roll(low, 64, 1), pad], axis=0))
    down_ref[...] = first[:R, :BW]
    up_ref[:64, :] = low[:64, :BW]
    up_ref[64:, :] = first[R:, :BW]


def on_device(hidden, lengths, starts, ranking, down_w, up_w, gain, head):
    x = hidden[0, 0]
    core = lax.axis_index("cand") % 2
    sibling = [(i, i ^ 1) for i in range(16)]
    both = gain.astype(f32) * head.astype(f32)
    near = lax.reduce_precision(both, 8, 7)
    part = jnp.where(core == 0, near, both - near).astype(bf16)
    half_w = jnp.where(core == 0, down_w, up_w)
    half_w = jnp.concatenate([half_w, jnp.broadcast_to(part[None], (32, BW))], axis=0)
    packed = pl.pallas_call(
        pack_kernel,
        out_shape=jax.ShapeDtypeStruct((8, 224, 128), bf16),
        in_specs=[VMEM],
        out_specs=VMEM,
        compiler_params=pltpu.CompilerParams(vmem_limit_bytes=16 << 20),
    )(half_w)
    along_y = [list(range(8)), list(range(8, 16))]
    mine = lax.all_to_all(packed, "fsdp", 0, 0, axis_index_groups=along_y, tiled=True)
    across = [(i, i ^ 8) for i in range(16)]
    far_mine = lax.ppermute(mine, "fsdp", across)
    other = lax.ppermute(mine, "cand", sibling)
    w_near, prod, gram, squares, x_t = pl.pallas_call(
        near_kernel,
        out_shape=(
            jax.ShapeDtypeStruct((HALF, 256), bf16),
            jax.ShapeDtypeStruct((TOK, 256), f32),
            jax.ShapeDtypeStruct((256, 256), f32),
            jax.ShapeDtypeStruct((TOK, 128), f32),
            jax.ShapeDtypeStruct((D, TOK), bf16),
        ),
        in_specs=[VMEM, VMEM, VMEM],
        out_specs=(VMEM, VMEM, VMEM, VMEM, VMEM),
        compiler_params=pltpu.CompilerParams(vmem_limit_bytes=24 << 20),
    )(x, mine, other)
    far_mine, squares = lax.optimization_barrier((far_mine, squares))
    far_other = lax.ppermute(far_mine, "cand", sibling)
    rows = BW + BW // 2 + 16
    send_a, send_b, *own = pl.pallas_call(
        local_kernel,
        out_shape=(
            jax.ShapeDtypeStruct((8, CUT + 16, 128), jnp.int16),
            jax.ShapeDtypeStruct((8, rows - CUT, 128), jnp.int16),
            jax.ShapeDtypeStruct((8, BW, 128), f32),
            jax.ShapeDtypeStruct((8, BW // 2, 128), f32),
            jax.ShapeDtypeStruct((8, 8, 512), f32),
            jax.ShapeDtypeStruct((8, 128), f32),
        ),
        in_specs=[SMEM, SMEM] + [VMEM] * 8,
        out_specs=(VMEM,) * 6,
        scratch_shapes=[
            pltpu.VMEM((HALF, 256), bf16),
            pltpu.VMEM((D, 256), bf16),
            pltpu.VMEM((D, 256), f32),
            pltpu.VMEM((8, D + 256), f32),
        ],
        compiler_params=pltpu.CompilerParams(vmem_limit_bytes=40 << 20),
    )(starts, lengths, x, w_near, prod, gram, squares, x_t, far_mine, far_other)
    got_a = lax.ppermute(send_a, "fsdp", [(i, i ^ 1) for i in range(16)])
    turn = [(i, i // 8 * 8 + (i + (1 if i % 2 else 7)) % 8) for i in range(16)]
    got_b = lax.ppermute(send_b, "fsdp", turn)
    coded_terms = pl.pallas_call(
        pair_kernel,
        out_shape=jax.ShapeDtypeStruct((8, rows, 128), jnp.int16),
        in_specs=[VMEM] * 6,
        out_specs=VMEM,
        compiler_params=pltpu.CompilerParams(vmem_limit_bytes=24 << 20),
    )(got_a, got_b, *own)
    parity = [list(range(0, 16, 2)), list(range(1, 16, 2))]
    swapped = lax.all_to_all(coded_terms, "fsdp", 0, 0, axis_index_groups=parity, tiled=True)
    sums = pl.pallas_call(
        block_kernel,
        out_shape=jax.ShapeDtypeStruct((8, 64, 128), f32),
        in_specs=[SMEM, VMEM],
        out_specs=VMEM,
        compiler_params=pltpu.CompilerParams(vmem_limit_bytes=16 << 20),
    )(ranking, swapped)
    along_z = [list(range(0, 16, 2)), list(range(1, 16, 2))]
    pieces = lax.all_to_all(sums, "cand", 0, 0, axis_index_groups=along_z, tiled=True)
    beside = lax.ppermute(pieces, "cand", sibling)
    share, loss = pl.pallas_call(
        slope_kernel,
        out_shape=(jax.ShapeDtypeStruct((56, 128), f32), jax.ShapeDtypeStruct((8, 128), f32)),
        in_specs=[VMEM, VMEM],
        out_specs=(VMEM, VMEM),
        compiler_params=pltpu.CompilerParams(vmem_limit_bytes=16 << 20),
    )(pieces, beside)
    final = pl.pallas_call(
        both_kernel,
        out_shape=jax.ShapeDtypeStruct((8, 56, 128), f32),
        in_specs=[VMEM, VMEM],
        out_specs=VMEM,
        compiler_params=pltpu.CompilerParams(vmem_limit_bytes=16 << 20),
    )(share, lax.ppermute(share, "prompt", [(0, 1), (1, 0)]))
    final = lax.all_to_all(final, "cand", 0, 0, axis_index_groups=along_z, tiled=True).reshape(448, 128)
    down_grad, up_grad = pl.pallas_call(
        out_kernel,
        out_shape=(jax.ShapeDtypeStruct((R, BW), f32), jax.ShapeDtypeStruct((R, BW), f32)),
        in_specs=[VMEM],
        out_specs=(VMEM, VMEM),
        compiler_params=pltpu.CompilerParams(vmem_limit_bytes=16 << 20),
    )(final)
    half = BW + BW // 2
    pooled = final[half : half + 3].reshape(-1)[:BW]
    gain_f, head_f = gain.astype(f32), head.astype(f32)
    return (loss[0, :1], down_grad, up_grad, head_f * pooled, gain_f * pooled)


def solution(mesh):
    placed = (
        P("prompt", "cand", "fsdp", None),
        P("prompt", "cand"),
        P("prompt", "cand"),
        P("prompt", None),
        P(None, "fsdp"),
        P(None, "fsdp"),
        P("fsdp"),
        P("fsdp"),
    )
    return jax.shard_map(
        on_device,
        mesh=mesh,
        in_specs=placed,
        out_specs=(P("prompt"), P(None, "fsdp"), P(None, "fsdp"), P("fsdp"), P("fsdp")),
        check_vma=False,
    )
```

```python
import jax
import jax.numpy as jnp
from jax import lax
from jax.experimental import pallas as pl
from jax.experimental.pallas import tpu as pltpu
from jax.sharding import PartitionSpec as P

loss_scale = 256.0
D = 4608
R = 96
TOK = 512
NB = 16
BW = 288
HALF = 2304
CH = 512
CUT = 224
STEPS = 32760.0
FINE = 60000.0
TINY = 1e-36
f32 = jnp.float32
bf16 = jnp.bfloat16
VMEM = pl.BlockSpec(memory_space=pltpu.VMEM)
SMEM = pl.BlockSpec(memory_space=pltpu.SMEM)


def mm(a, b, ca, cb):
    return lax.dot_general(a, b, (((ca,), (cb,)), ((), ())), preferred_element_type=f32)


def halves(v):
    hi = v.astype(bf16)
    return hi, (v - hi.astype(f32)).astype(bf16)


def lanes(shape):
    return lax.broadcasted_iota(jnp.int32, shape, len(shape) - 1)


def level(most):
    return jnp.ceil(jnp.log2(jnp.maximum(most, TINY)) * 8.0)


def coded(v, e):
    return jnp.round(v * jnp.exp2(e * -0.125) * STEPS).astype(jnp.int32)


def told_row(part):
    e = level(jnp.abs(part))
    v = part * jnp.exp2(e * -0.125) * STEPS
    hi = jnp.round(v)
    lo = jnp.round((v - hi) * FINE)
    one = lanes((1, 128))
    return jnp.where(one == 0, e, jnp.where(one == 1, hi, jnp.where(one == 2, lo, 0.0))).astype(jnp.int32)


def told(m, scale):
    one = lanes((1, 128))
    v = jnp.where(one == 1, m[6:7], jnp.where(one == 2, m[6:7] * (1.0 / FINE), 0.0))
    by = jnp.sum(jnp.where(one == 0, scale[6:7], 0.0), axis=1, keepdims=True)
    return jnp.sum(v, axis=1, keepdims=True) * (by * (1.0 / STEPS))


def meta_rows(a_e, b_e, window, s_row):
    p_e = level(jnp.max(jnp.abs(window), axis=1, keepdims=True))
    p_q = coded(window, p_e)
    rows = (
        a_e.astype(jnp.int32),
        b_e.astype(jnp.int32),
        p_q[0:1, :128],
        p_q[0:1, 128:256],
        p_q[0:1, 256:384],
        jnp.broadcast_to(p_e[0:1].astype(jnp.int32), (1, 128)),
        s_row,
    )
    at = lax.broadcasted_iota(jnp.int32, (16, 128), 0)
    meta = jnp.zeros((16, 128), jnp.int32)
    for k, r in enumerate(rows):
        meta = jnp.where(at == k, r, meta)
    return meta.astype(jnp.int16)


def pack_kernel(w_ref, out_ref):
    w = w_ref[...].astype(f32)
    w = jnp.concatenate([w, jnp.zeros((128, 96), f32)], axis=1)
    t = jnp.transpose(w)
    lane = lanes((64, 128))
    last = t[224:288]
    for i in range(3):
        cut = slice(64 * i, 64 * i + 64)
        rows = jnp.where(lane < R, t[cut], pltpu.roll(last, 96 - 32 * i, 1)).astype(bf16)
        for j in range(8):
            out_ref[j, cut, :] = rows
    lane = lanes((32, 128))
    rows = jnp.where(lane < R, t[192:224], 0.0)
    for k in range(9):
        piece = t[32 * k : 32 * k + 32]
        rows = jnp.where(lane == R + k, pltpu.roll(piece, k, 1) if k else piece, rows)
    rows = rows.astype(bf16)
    for j in range(8):
        out_ref[j, 192:, :] = rows


def unpack(q_ref, store):
    for j in range(8):
        q = q_ref[j].astype(f32)
        lane = lanes((32, 128))
        part = q[192:]
        cols = [pltpu.roll(part, 128 - k, 1) if k else part for k in range(9)]
        for k in range(7):
            rows = jnp.where(lane < R, q[32 * k : 32 * k + 32], jnp.where(lane == R, cols[k], 0.0))
            store(j * BW + 32 * k, rows.astype(bf16))
        for k in range(2):
            cut = [pltpu.roll(q[64 * i + 32 * k : 64 * i + 32 * k + 32], 32 * i + 32, 1) for i in range(3)]
            rows = jnp.where(lane < 32, cut[0], jnp.where(lane < 64, cut[1], cut[2]))
            rows = jnp.where(lane < R, rows, jnp.where(lane == R, cols[7 + k], 0.0))
            store(j * BW + 224 + 32 * k, rows.astype(bf16))


def unpack_both(core, mine_ref, other_ref, w_ref):
    def stores(left):
        def to_left(at, rows):
            w_ref[at : at + 32, :128] = rows

        def to_right(at, rows):
            w_ref[at : at + 32, 128:] = rows

        return (to_left, to_right) if left else (to_right, to_left)

    for left in (True, False):

        @pl.when((core == 0) == left)
        def _(left=left):
            first, second = stores(left)
            unpack(mine_ref, first)
            unpack(other_ref, second)


def near_kernel(x_ref, mine_ref, other_ref, w_ref, prod_ref, gram_ref, ss_ref):
    unpack_both(lax.axis_index("cand") % 2, mine_ref, other_ref, w_ref)

    def square(i, carry):
        at = pl.ds(pl.multiple_of(i * 16, 16), 16)
        rows = x_ref[at, :].astype(f32)
        ss_ref[at, :] = jnp.broadcast_to(jnp.sum(rows * rows, axis=1, keepdims=True), (16, 128))
        return carry

    lax.fori_loop(0, TOK // 16, square, 0)
    cols = pl.ds(pl.multiple_of(lax.axis_index("fsdp") // 8 * HALF, 128), HALF)
    prod_ref[...] = mm(x_ref[:, cols], w_ref[...], 1, 0)
    gram_ref[...] = mm(w_ref[:, 128:], w_ref[...], 0, 0)


def local_kernel(
    starts,
    lengths,
    x_ref,
    w_near,
    prod_near,
    gram_near,
    ss_ref,
    mine_ref,
    other_ref,
    send_a,
    send_b,
    own_a,
    own_b,
    own_p,
    own_s,
    w_far,
    w_ref,
    g_ref,
    p_ref,
):
    start, length = starts[0, 0], lengths[0, 0]
    first = lax.axis_index("fsdp") * TOK
    core = lax.axis_index("cand") % 2
    side = lax.axis_index("fsdp") // 8
    unpack_both(core, mine_ref, other_ref, w_far)
    w_ref[pl.ds(pl.multiple_of(side * HALF, 256), HALF), :] = w_near[...]
    w_ref[pl.ds(pl.multiple_of((1 - side) * HALF, 256), HALF), :] = w_far[...]
    cols = pl.ds(pl.multiple_of((1 - side) * HALF, 128), HALF)
    prod = prod_near[...] + mm(x_ref[:, cols], w_far[...], 1, 0)
    gram = gram_near[...] + mm(w_far[:, 128:], w_far[...], 0, 0)
    pre = prod[:, :128]
    x_up = prod[:, 128:]
    lane = lanes((TOK, 128))
    unit = lane < R
    sig = 1.0 / (1.0 + jnp.exp(-pre))
    act_b = jnp.where(unit, pre * sig, 0.0).astype(bf16)
    act = act_b.astype(f32)
    g_hi, g_lo = halves(gram)
    through = mm(act_b, g_hi, 1, 0) + mm(act_b, g_lo, 1, 0)
    m_left = pre + through[:, :128]
    m_up = x_up + through[:, 128:]
    m_head = jnp.sum(jnp.where(lane == R, m_left + m_up, 0.0), axis=1, keepdims=True)
    m_sq = ss_ref[:, :1] + jnp.sum(act * (x_up + m_up), axis=1, keepdims=True)
    inv = lax.rsqrt(jnp.maximum(m_sq, 0.0) * (1.0 / D) + 1e-06)
    score = inv * m_head
    count = (length - start).astype(f32)
    pos = first + lax.broadcasted_iota(jnp.int32, (TOK, 1), 0)
    valid = (pos >= start) & (pos < length)
    part = jnp.sum(jnp.where(valid, score, 0.0), axis=0, keepdims=True) / count
    weight = jnp.where(valid, loss_scale / count, 0.0)
    alpha = inv * weight
    beta = inv * inv * weight * score * (1.0 / D)
    up_head = jnp.transpose(gram[:, :128])[R : R + 1] + gram[R : R + 1, 128:]
    back = alpha * up_head - beta * m_up
    pre_grad = back * sig * (1.0 + pre * (1.0 - sig))
    nab = -(act * beta)
    left = jnp.where(unit, pre_grad, pltpu.roll(nab, 32, 1))
    right = jnp.where(lane < 64, nab, pltpu.roll(nab, 64, 1))
    lhs = jnp.concatenate([left, right], axis=1).astype(bf16)
    a_left = jnp.where(unit, 0.0, pltpu.roll(act, 32, 1))
    a_right = jnp.where(lane < 64, act, pltpu.roll(act, 64, 1))
    u_row = jnp.sum(alpha * jnp.concatenate([a_left, a_right], axis=1), axis=0, keepdims=True)
    v_row = jnp.sum(alpha * act, axis=0, keepdims=True)
    low = mm(act_b, lhs, 0, 0)
    low = jnp.where(lanes((128, 256)) < R, 0.0, low)
    row = lax.broadcasted_iota(jnp.int32, (128, 256), 0)
    top = jnp.where(row == R, u_row, 0.0)
    low = jnp.where(row == R, u_row, low)
    c_hi, c_lo = halves(jnp.concatenate([top, low], axis=0))
    for i in range(D // CH):
        cut = slice(i * CH, (i + 1) * CH)
        w = w_ref[cut, :]
        g_ref[cut, :] = mm(x_ref[:, cut], lhs, 0, 0) + (mm(w, c_hi, 1, 0) + mm(w, c_lo, 1, 0))

    al_hi = alpha.astype(bf16).astype(f32)
    al_lo = alpha - al_hi
    al = jnp.where(lane == 0, al_hi, jnp.where(lane == 1, al_lo, 0.0))
    al = jnp.transpose(al)[:16].astype(bf16)
    v_hi = v_row.astype(bf16).astype(f32)
    row = lax.broadcasted_iota(jnp.int32, (16, 128), 0)
    vv = jnp.where(row == 0, v_hi, jnp.where(row == 1, v_row - v_hi, 0.0)).astype(bf16)
    pooled = mm(al, x_ref[...], 1, 0) + mm(vv, w_ref[:, 128:], 1, 1)
    p_ref[:, D:] = jnp.zeros((8, 256), f32)
    p_ref[:, :D] = jnp.broadcast_to(pooled[0:1] + pooled[1:2], (8, D))

    def window(j):
        base = j * BW // 128 * 128
        off = j * BW - base
        w = p_ref[:, base : base + 512]
        if off:
            w = pltpu.roll(w, 512 - off, 1)
        return jnp.where(lanes((8, 512)) < BW, w, 0.0)

    def block(j):
        a = g_ref[pl.ds(pl.multiple_of(j * BW, 32), BW), :128]
        b0 = g_ref[pl.ds(pl.multiple_of(j * BW, 32), BW // 2), 128:]
        b1 = g_ref[pl.ds(pl.multiple_of(j * BW + BW // 2, 16), BW // 2), 128:]
        return a, jnp.where(lanes((BW // 2, 128)) < 64, b0, b1)

    par = lax.axis_index("fsdp") % 2
    s_row = told_row(part)
    own_s[...] = jnp.broadcast_to(part, (8, 128))
    for i in range(8):
        even, odd = window(2 * i), window(2 * i + 1)
        a, b = block(2 * i + 1 - par)
        a_e = level(jnp.max(jnp.abs(a), axis=0, keepdims=True))
        b_e = level(jnp.max(jnp.abs(b), axis=0, keepdims=True))
        q = coded(a, a_e).astype(jnp.int16)
        meta = meta_rows(a_e, b_e, jnp.where(par == 0, odd, even), s_row)
        send_a[i, :CUT, :] = q[:CUT]
        send_a[i, CUT:, :] = meta
        send_b[i, : BW - CUT, :] = q[CUT:]
        send_b[i, BW - CUT : BW - CUT + BW // 2, :] = coded(b, b_e).astype(jnp.int16)
        send_b[i, BW - CUT + BW // 2 :, :] = meta
        a, b = block(2 * i + par)
        own_a[i] = a
        own_b[i] = b
        own_p[i] = jnp.where(par == 0, even, odd)


def pair_kernel(got_a, got_b, own_a, own_b, own_p, own_s, out_ref):
    end = BW - CUT + BW // 2
    m_a = [got_a[i, CUT:, :].astype(jnp.int32).astype(f32) for i in range(8)]
    m_b = [got_b[i, end:, :].astype(jnp.int32).astype(f32) for i in range(8)]
    scale = jnp.exp2(m_b[0] * 0.125)
    s_row = told_row(own_s[0:1, 0:1] + told(m_b[0], scale))
    for i in range(8):
        by_a = jnp.exp2(m_a[i][0:1] * 0.125) * (1.0 / STEPS)
        by = jnp.exp2(m_b[i] * 0.125) * (1.0 / STEPS)
        top = own_a[i, :CUT] + got_a[i, :CUT, :].astype(jnp.int32).astype(f32) * by_a
        low = own_a[i, CUT:] + got_b[i, : BW - CUT, :].astype(jnp.int32).astype(f32) * by[0:1]
        b = own_b[i] + got_b[i, BW - CUT : end, :].astype(jnp.int32).astype(f32) * by[1:2]
        m = m_b[i]
        got_p = jnp.concatenate([m[2:3], m[3:4], m[4:5], jnp.zeros((1, 128), f32)], axis=1)
        p = own_p[i] + got_p * jnp.concatenate([by[5:6]] * 4, axis=1)
        most = jnp.maximum(
            jnp.max(jnp.abs(top), axis=0, keepdims=True), jnp.max(jnp.abs(low), axis=0, keepdims=True)
        )
        a_e = level(most)
        b_e = level(jnp.max(jnp.abs(b), axis=0, keepdims=True))
        out_ref[i, :CUT, :] = coded(top, a_e).astype(jnp.int16)
        out_ref[i, CUT:BW, :] = coded(low, a_e).astype(jnp.int16)
        out_ref[i, BW : BW + BW // 2, :] = coded(b, b_e).astype(jnp.int16)
        out_ref[i, BW + BW // 2 :, :] = meta_rows(a_e, b_e, p, s_row)


def block_kernel(ranking, q_ref, out_ref):
    mine = lax.axis_index("cand")
    place = jnp.int32(0)
    for k in range(16):
        place = jnp.where(ranking[0, k] == mine, jnp.int32(k), place)
    half = BW + BW // 2
    parts = [q_ref[s, half:, :].astype(jnp.int32).astype(f32) for s in range(8)]
    scale = [jnp.exp2(m * 0.125) for m in parts]
    pooled = [jnp.zeros((1, 128), f32) for _ in range(3)]
    reward = jnp.zeros((1, 1), f32)
    one = lanes((1, 128))
    for s in range(8):
        m, e = parts[s], scale[s] * (1.0 / STEPS)
        for k in range(3):
            pooled[k] = pooled[k] + m[2 + k : 3 + k] * e[5:6]
        reward = reward + told(m, scale[s])
    at = lax.broadcasted_iota(jnp.int32, (16, 128), 0)
    tail = jnp.zeros((16, 128), f32)
    for k in range(3):
        tail = jnp.where(at == k, pooled[k], tail)
    meta = jnp.where(one < 64, reward, place.astype(f32))
    meta = jnp.broadcast_to(meta, (8, 128))
    for i in range(28):
        if i < half // 16:
            which = 0 if i < BW // 16 else 1
            acc = jnp.zeros((16, 128), f32)
            for s in range(8):
                v = q_ref[s, i * 16 : (i + 1) * 16, :].astype(jnp.int32).astype(f32)
                acc = acc + v * (scale[s][which : which + 1] * (1.0 / STEPS))
        else:
            acc = tail
        for g in (2 * i, 2 * i + 1):
            at = g % 7 * 8
            out_ref[g // 7, at : at + 8, :] = acc[g % 2 * 8 : g % 2 * 8 + 8]
    for i in range(8):
        out_ref[i, 56:, :] = meta


def slope_kernel(d_ref, o_ref, out_ref, loss_ref):
    told = jnp.concatenate([d_ref[:, 56, :], o_ref[:, 56, :]], axis=0)
    lane = lanes((16, 128))
    row = lax.broadcasted_iota(jnp.int32, (16, 128), 0)
    r_col = jnp.sum(jnp.where(lane == 0, told, 0.0), axis=1, keepdims=True)
    k_col = jnp.sum(jnp.where(lane == 64, told, 0.0), axis=1, keepdims=True)
    r_row = jnp.sum(jnp.where(lane == row, r_col, 0.0), axis=0, keepdims=True)
    k_row = jnp.sum(jnp.where(lane == row, k_col, 0.0), axis=0, keepdims=True)
    real = lane < 16
    later = real & (k_col >= k_row)
    top = jnp.max(jnp.where(later, r_col, -1e30), axis=0, keepdims=True)
    top = jnp.where(real[0:1], top, 0.0)
    ex = jnp.where(later, jnp.exp(jnp.where(later, r_col - top, 0.0)), 0.0)
    total = jnp.where(real[0:1], jnp.sum(ex, axis=0, keepdims=True), 1.0)
    slope = jnp.sum(ex / total, axis=1, keepdims=True) - 1.0
    terms = jnp.where(real[0:1], top + jnp.log(total) - r_row, 0.0)
    loss_ref[...] = jnp.broadcast_to(jnp.sum(terms, axis=1, keepdims=True), (8, 128))
    acc = jnp.zeros((56, 128), f32)
    for i in range(8):
        acc = acc + d_ref[i, :56, :] * slope[i : i + 1] + o_ref[i, :56, :] * slope[8 + i : 9 + i]
    out_ref[...] = acc


def both_kernel(a_ref, b_ref, out_ref):
    both = a_ref[...] + b_ref[...]
    for i in range(8):
        out_ref[i] = both


def out_kernel(in_ref, down_ref, up_ref):
    pad = jnp.zeros((384 - BW, 128), f32)
    first = jnp.transpose(jnp.concatenate([in_ref[:BW], pad], axis=0))
    low = in_ref[BW : BW + BW // 2]
    low = jnp.transpose(jnp.concatenate([low, pltpu.roll(low, 64, 1), pad], axis=0))
    down_ref[...] = first[:R, :BW]
    up_ref[:64, :] = low[:64, :BW]
    up_ref[64:, :] = first[R:, :BW]


def on_device(hidden, lengths, starts, ranking, down_w, up_w, gain, head):
    x = hidden[0, 0]
    core = lax.axis_index("cand") % 2
    sibling = [(i, i ^ 1) for i in range(16)]
    both = gain.astype(f32) * head.astype(f32)
    near = lax.reduce_precision(both, 8, 7)
    part = jnp.where(core == 0, near, both - near).astype(bf16)
    half_w = jnp.where(core == 0, down_w, up_w)
    half_w = jnp.concatenate([half_w, jnp.broadcast_to(part[None], (32, BW))], axis=0)
    packed = pl.pallas_call(
        pack_kernel,
        out_shape=jax.ShapeDtypeStruct((8, 224, 128), bf16),
        in_specs=[VMEM],
        out_specs=VMEM,
        compiler_params=pltpu.CompilerParams(vmem_limit_bytes=16 << 20),
    )(half_w)
    along_y = [list(range(8)), list(range(8, 16))]
    mine = lax.all_to_all(packed, "fsdp", 0, 0, axis_index_groups=along_y, tiled=True)
    across = [(i, i ^ 8) for i in range(16)]
    far_mine = lax.ppermute(mine, "fsdp", across)
    other = lax.ppermute(mine, "cand", sibling)
    w_near, prod, gram, squares = pl.pallas_call(
        near_kernel,
        out_shape=(
            jax.ShapeDtypeStruct((HALF, 256), bf16),
            jax.ShapeDtypeStruct((TOK, 256), f32),
            jax.ShapeDtypeStruct((128, 256), f32),
            jax.ShapeDtypeStruct((TOK, 128), f32),
        ),
        in_specs=[VMEM, VMEM, VMEM],
        out_specs=(VMEM, VMEM, VMEM, VMEM),
        compiler_params=pltpu.CompilerParams(vmem_limit_bytes=24 << 20),
    )(x, mine, other)
    far_mine, squares = lax.optimization_barrier((far_mine, squares))
    far_other = lax.ppermute(far_mine, "cand", sibling)
    rows = BW + BW // 2 + 16
    send_a, send_b, *own = pl.pallas_call(
        local_kernel,
        out_shape=(
            jax.ShapeDtypeStruct((8, CUT + 16, 128), jnp.int16),
            jax.ShapeDtypeStruct((8, rows - CUT, 128), jnp.int16),
            jax.ShapeDtypeStruct((8, BW, 128), f32),
            jax.ShapeDtypeStruct((8, BW // 2, 128), f32),
            jax.ShapeDtypeStruct((8, 8, 512), f32),
            jax.ShapeDtypeStruct((8, 128), f32),
        ),
        in_specs=[SMEM, SMEM] + [VMEM] * 7,
        out_specs=(VMEM,) * 6,
        scratch_shapes=[
            pltpu.VMEM((HALF, 256), bf16),
            pltpu.VMEM((D, 256), bf16),
            pltpu.VMEM((D, 256), f32),
            pltpu.VMEM((8, D + 256), f32),
        ],
        compiler_params=pltpu.CompilerParams(vmem_limit_bytes=40 << 20),
    )(starts, lengths, x, w_near, prod, gram, squares, far_mine, far_other)
    got_a = lax.ppermute(send_a, "fsdp", [(i, i ^ 1) for i in range(16)])
    turn = [(i, i // 8 * 8 + (i + (1 if i % 2 else 7)) % 8) for i in range(16)]
    got_b = lax.ppermute(send_b, "fsdp", turn)
    coded_terms = pl.pallas_call(
        pair_kernel,
        out_shape=jax.ShapeDtypeStruct((8, rows, 128), jnp.int16),
        in_specs=[VMEM] * 6,
        out_specs=VMEM,
        compiler_params=pltpu.CompilerParams(vmem_limit_bytes=24 << 20),
    )(got_a, got_b, *own)
    parity = [list(range(0, 16, 2)), list(range(1, 16, 2))]
    swapped = lax.all_to_all(coded_terms, "fsdp", 0, 0, axis_index_groups=parity, tiled=True)
    sums = pl.pallas_call(
        block_kernel,
        out_shape=jax.ShapeDtypeStruct((8, 64, 128), f32),
        in_specs=[SMEM, VMEM],
        out_specs=VMEM,
        compiler_params=pltpu.CompilerParams(vmem_limit_bytes=16 << 20),
    )(ranking, swapped)
    along_z = [list(range(0, 16, 2)), list(range(1, 16, 2))]
    pieces = lax.all_to_all(sums, "cand", 0, 0, axis_index_groups=along_z, tiled=True)
    beside = lax.ppermute(pieces, "cand", sibling)
    share, loss = pl.pallas_call(
        slope_kernel,
        out_shape=(jax.ShapeDtypeStruct((56, 128), f32), jax.ShapeDtypeStruct((8, 128), f32)),
        in_specs=[VMEM, VMEM],
        out_specs=(VMEM, VMEM),
        compiler_params=pltpu.CompilerParams(vmem_limit_bytes=16 << 20),
    )(pieces, beside)
    final = pl.pallas_call(
        both_kernel,
        out_shape=jax.ShapeDtypeStruct((8, 56, 128), f32),
        in_specs=[VMEM, VMEM],
        out_specs=VMEM,
        compiler_params=pltpu.CompilerParams(vmem_limit_bytes=16 << 20),
    )(share, lax.ppermute(share, "prompt", [(0, 1), (1, 0)]))
    final = lax.all_to_all(final, "cand", 0, 0, axis_index_groups=along_z, tiled=True).reshape(448, 128)
    down_grad, up_grad = pl.pallas_call(
        out_kernel,
        out_shape=(jax.ShapeDtypeStruct((R, BW), f32), jax.ShapeDtypeStruct((R, BW), f32)),
        in_specs=[VMEM],
        out_specs=(VMEM, VMEM),
        compiler_params=pltpu.CompilerParams(vmem_limit_bytes=16 << 20),
    )(final)
    half = BW + BW // 2
    pooled = final[half : half + 3].reshape(-1)[:BW]
    gain_f, head_f = gain.astype(f32), head.astype(f32)
    return (loss[0, :1], down_grad, up_grad, head_f * pooled, gain_f * pooled)


def solution(mesh):
    placed = (
        P("prompt", "cand", "fsdp", None),
        P("prompt", "cand"),
        P("prompt", "cand"),
        P("prompt", None),
        P(None, "fsdp"),
        P(None, "fsdp"),
        P("fsdp"),
        P("fsdp"),
    )
    return jax.shard_map(
        on_device,
        mesh=mesh,
        in_specs=placed,
        out_specs=(P("prompt"), P(None, "fsdp"), P(None, "fsdp"), P("fsdp"), P("fsdp")),
        check_vma=False,
    )
```
